32 devices in a mesh: seq: 8 (over z, x), head: 4 (over y, core).
Axes of the slice: x: 2, y: 2, z: 4, core: 2. Of those that a mesh axis runs over, the one named last changes fastest.
Arguments:
- queries: bfloat16 [4096, 4096], P('seq', 'head'), may hold values from -6 to 6
- key_rows: bfloat16 [4096, 4096], P('seq', 'head'), may hold values from -6 to 6
- value_rows: bfloat16 [4096, 4096], P('seq', 'head'), may hold values from -18 to 18
- out_grad: bfloat16 [4096, 4096], P('seq', 'head'), may hold values from -6 to 6
- log_decay: float32 [32, 4096], P('head', 'seq'), may hold values from -0.6 to 0
Outputs:
- query_gradient: bfloat16 [4096, 4096], P('seq', 'head')
- key_grad: bfloat16 [4096, 4096], P('seq', 'head')
- value_grad: bfloat16 [4096, 4096], P('seq', 'head')
The draws below stay inside these ranges and needn't reach their ends.
All inputs are finite; a program needn't handle non-finite values.
Results may differ from the reference program's by a relative error of at most 0.006.
Values sent between devices are 32-bit elements; how exact they have to be, the bound alone decides.
A program may use at most 64 MiB of HBM per device.

```python
import jax
import jax.numpy as jnp
from jax import lax

HEAD_COUNT = 32
DH = 128
BLOCK = 128
TOKEN_COUNT = 4096


def draw_log_decay(key, part):
    key_sequence = jax.random.split(key, 6)
    fast_share = 0.5
    fast_heads = jax.random.bernoulli(key_sequence[0], fast_share, (HEAD_COUNT,))
    fast_rate = jnp.exp(jax.random.uniform(key_sequence[1], (HEAD_COUNT,), jnp.float32, jnp.log(1.0 / 50.0), jnp.log(1.0 / 30.0)))
    slow_rate = jax.random.uniform(key_sequence[2], (HEAD_COUNT,), jnp.float32, 0.05, 0.4) / TOKEN_COUNT
    head_rate = jnp.where(fast_heads, fast_rate, slow_rate)
    factor = jnp.exp(jax.random.uniform(key_sequence[3], (HEAD_COUNT, TOKEN_COUNT), jnp.float32, jnp.log(0.5), jnp.log(2.0)))
    decay_logarithm = -head_rate[:, None] * factor
    spike_positions = jax.random.randint(key_sequence[4], (3,), 0, TOKEN_COUNT)
    token_positions = jnp.arange(TOKEN_COUNT, dtype=jnp.int32)
    spike_selected = jnp.any(token_positions[None, :] == spike_positions[:, None], axis=0)
    spike_retained = jax.random.uniform(key_sequence[5], (HEAD_COUNT, TOKEN_COUNT), jnp.float32, 0.55, 0.8)
    decay_logarithm = jnp.where(spike_selected[None, :], jnp.log(spike_retained), decay_logarithm)
    return decay_logarithm.astype(jnp.float32)


def draw_value_rows(key, part):
    key_sequence = jax.random.split(key, 2)
    head_scale = jnp.exp(jax.random.uniform(key_sequence[0], (HEAD_COUNT,), jnp.float32, jnp.log(0.3), jnp.log(3.0)))
    column_scale = jnp.repeat(head_scale, DH)
    base = jnp.clip(jax.random.normal(key_sequence[1], (TOKEN_COUNT, HEAD_COUNT * DH), jnp.float32), -6.0, 6.0)
    return (base * column_scale[None, :]).astype(jnp.bfloat16)


def level_of(own_key, extent, shards, least, high):
    gain, own = 1.0, jax.random.fold_in(own_key, 6)
    for axis_at, shards_of in shards:
        draws = jnp.exp(jax.random.uniform(jax.random.fold_in(own, axis_at), (shards_of,), jnp.float32, least / len(shards), high / len(shards)))
        gain = gain * jnp.repeat(draws, extent[axis_at] // shards_of).reshape([-1 if axis == axis_at else 1 for axis in range(len(extent))])
    return gain


def normal_values(rng, extent, spread, reach, cuts=(), kind=jnp.bfloat16):
    result = jax.random.normal(rng, extent, jnp.float32) * spread
    if len(cuts) > 0:
        result = level_of(rng, extent, cuts, -0.22, 0.18) * result
    return jnp.clip(result, min=-reach, max=reach).astype(kind)


def setup_inputs(seed: int = 0) -> dict:
    key_list = jax.random.split(jax.random.key(seed), 6)
    queries = normal_values(key_list[0], (TOKEN_COUNT, HEAD_COUNT * DH), 1.0, 6.0, ((0, 8), (1, 4)))
    key_rows = normal_values(key_list[1], (TOKEN_COUNT, HEAD_COUNT * DH), 1.0, 6.0, ((0, 8), (1, 4)))
    value_rows = draw_value_rows(jax.random.fold_in(key_list[5], 71), 0)
    out_grad = normal_values(key_list[3], (TOKEN_COUNT, HEAD_COUNT * DH), 1.0, 6.0, ((0, 8), (1, 4)))
    log_decay = draw_log_decay(jax.random.fold_in(key_list[5], 71), 0)
    return {"queries": queries, "key_rows": key_rows, "value_rows": value_rows, "out_grad": out_grad, "log_decay": log_decay}


epsilon = 1e-06

def rounded(array):
    return lax.optimization_barrier(array.astype(jnp.bfloat16)).astype(jnp.float32)

def pairwise_product(form, left, right):
    return jnp.einsum(form, left, right, precision=lax.Precision.HIGHEST)

def advance(running, block_item):
    block_total, block_term = block_item
    return (jnp.exp(block_total) * running + block_term, running)

def head_columns(array, head_id):
    blocks = TOKEN_COUNT // BLOCK
    column = (head_id * DH).astype(jnp.int32)
    picked = lax.dynamic_slice_in_dim(array, column, DH, 1)
    return picked.astype(jnp.float32).reshape(blocks, BLOCK, DH)

def head_parts(head_id, queries, key_rows, value_rows, log_decay):
    blocks = TOKEN_COUNT // BLOCK
    query_block_rows = head_columns(queries, head_id)
    key_blocks = head_columns(key_rows, head_id)
    value_block_rows = head_columns(value_rows, head_id)
    decay_row = lax.dynamic_index_in_dim(log_decay, head_id, 0, keepdims=False).reshape(blocks, BLOCK)
    inside_block_mask = jnp.cumsum(decay_row, axis=1)
    totals = inside_block_mask[:, -1]
    token_positions = jnp.arange(BLOCK, dtype=jnp.int32)
    causal = (token_positions[:, None] >= token_positions[None, :]).astype(jnp.float32)
    exponent = inside_block_mask[:, :, None] - inside_block_mask[:, None, :]
    decay_mask = jnp.exp(jnp.minimum(exponent, 0.0)) * causal
    scores = pairwise_product('nid,njd->nij', query_block_rows, key_blocks)
    attention_weights = rounded(scores * decay_mask)
    to_end = jnp.exp(totals[:, None] - inside_block_mask)
    keys_scaled = rounded(to_end[:, :, None] * key_blocks)
    block_terms = pairwise_product('njd,nje->nde', keys_scaled, value_block_rows)
    empty_state = jnp.zeros((DH, DH), jnp.float32)
    final_state, states = lax.scan(advance, empty_state, (totals, block_terms))
    backward_state = rounded(states)
    attention_output = pairwise_product('nij,njd->nid', attention_weights, value_block_rows)
    attention_output = attention_output + jnp.exp(inside_block_mask)[:, :, None] * pairwise_product('hrk,hkc->hrc', query_block_rows, backward_state)
    return (query_block_rows, key_blocks, value_block_rows, inside_block_mask, totals, decay_mask, attention_weights, backward_state, to_end, attention_output)

def reference(queries, key_rows, value_rows, out_grad, log_decay):
    head_ids = jnp.arange(HEAD_COUNT, dtype=jnp.int32)
    total_width = HEAD_COUNT * DH

    def head_stats(head_id):
        parts = head_parts(head_id, queries, key_rows, value_rows, log_decay)
        attention_output = parts[-1]
        grad_blocks = head_columns(out_grad, head_id)
        return (lax.optimization_barrier(jnp.sum(attention_output * attention_output, axis=2)), lax.optimization_barrier(jnp.sum(grad_blocks * attention_output, axis=2)))
    squares, crosses = lax.map(head_stats, head_ids)
    inv_rms = lax.rsqrt(lax.optimization_barrier(jnp.sum(squares, axis=0)) / total_width + epsilon)
    mean_cross = inv_rms * lax.optimization_barrier(jnp.sum(crosses, axis=0)) / total_width

    def head_grads(head_id):
        parts = head_parts(head_id, queries, key_rows, value_rows, log_decay)
        query_block_rows, key_blocks, value_block_rows, inside_block_mask, totals, decay_mask, attention_weights, backward_state, to_end, attention_output = parts
        grad_blocks = head_columns(out_grad, head_id)
        normed = attention_output * inv_rms[:, :, None]
        attention_gradient = rounded(inv_rms[:, :, None] * (grad_blocks - normed * mean_cross[:, :, None]))
        score_gradient = pairwise_product('spa,soa->spo', attention_gradient, value_block_rows)
        grad_probs = rounded(score_gradient * decay_mask)
        query_gradient = pairwise_product('nij,njd->nid', grad_probs, key_blocks)
        query_gradient = query_gradient + jnp.exp(inside_block_mask)[:, :, None] * pairwise_product('tjg,tog->tjo', attention_gradient, backward_state)
        key_intra = pairwise_product('nij,nid->njd', grad_probs, query_block_rows)
        value_within_block = pairwise_product('osx,osg->oxg', attention_weights, attention_gradient)
        scaled_query_rows = rounded(jnp.exp(inside_block_mask)[:, :, None] * query_block_rows)
        backward_terms = pairwise_product('gjh,gjb->ghb', scaled_query_rows, attention_gradient)
        empty_state = jnp.zeros((DH, DH), jnp.float32)
        final_state, back_states = lax.scan(advance, empty_state, (totals, backward_terms), reverse=True)
        back_b = rounded(back_states)
        key_grad = key_intra + to_end[:, :, None] * pairwise_product('nje,nde->njd', value_block_rows, back_b)
        value_grad = value_within_block + to_end[:, :, None] * pairwise_product('njd,nde->nje', key_blocks, back_b)
        return (query_gradient.reshape(TOKEN_COUNT, DH).astype(jnp.bfloat16), key_grad.reshape(TOKEN_COUNT, DH).astype(jnp.bfloat16), value_grad.reshape(TOKEN_COUNT, DH).astype(jnp.bfloat16))
    query_all, key_all, value_all = lax.map(head_grads, head_ids)

    def arrange(stacked):
        return jnp.transpose(stacked, (1, 0, 2)).reshape(TOKEN_COUNT, HEAD_COUNT * DH)
    return (arrange(query_all), arrange(key_all), arrange(value_all))
```

```python
import functools

import jax
import jax.numpy as jnp
from jax import lax
from jax.experimental import pallas as pl
from jax.experimental.pallas import tpu as pltpu
from jax.sharding import PartitionSpec as P

HEAD_COUNT = 32
DH = 128
BLOCK = 128
EPSILON = 1e-06

f32 = jnp.float32
bf16 = jnp.bfloat16


def dot(left, right, left_dim, right_dim):
    return lax.dot_general(
        left, right, (((left_dim,), (right_dim,)), ((), ())), preferred_element_type=f32
    )


def kernel(
    n_seq,
    n_head,
    q_hbm,
    k_hbm,
    v_hbm,
    g_hbm,
    ld_hbm,
    qo_hbm,
    ko_hbm,
    vo_hbm,
    q_ref,
    k_ref,
    v_ref,
    g_ref,
    ld_ref,
    within_ref,
    total_ref,
    dec_ref,
    shard_dec_ref,
    terms,
    mask_ref,
    grow_ref,
    end_ref,
    attn_ref,
    probs_ref,
    ag_ref,
    state_ref,
    ki_ref,
    vi_ref,
    slab,
    pair_in,
    chain_in,
    chain_out,
    pair_out,
    incoming,
    acc_ref,
    stat_out,
    stat_in,
    row_ref,
    q_out,
    k_out,
    v_out,
    load_sem,
    pair_send,
    pair_recv,
    chain_send,
    chain_recv,
    fin_send,
    fin_recv,
    stat_send,
    stat_recv,
    out_sem,
):
    heads = ld_ref.shape[0]
    blocks = ld_ref.shape[1] // BLOCK
    half = heads // 2
    groups = n_seq // 2
    rank = lax.axis_index("seq")
    col = lax.axis_index("head")
    x = lax.rem(rank, 2)
    z = rank // 2
    partner = rank + 1 - 2 * x

    loads = [
        pltpu.make_async_copy(src, dst, load_sem.at[at])
        for at, (src, dst) in enumerate(
            [(ld_hbm, ld_ref), (k_hbm, k_ref), (v_hbm, v_ref), (q_hbm, q_ref), (g_hbm, g_ref)]
        )
    ]
    for load in loads:
        load.start()

    barrier = pltpu.get_barrier_semaphore()
    pl.semaphore_signal(barrier, inc=1, device_id={"seq": partner})

    @pl.when(z > 0)
    def _():
        pl.semaphore_signal(barrier, inc=1, device_id={"seq": rank - 2})

    @pl.when(z < groups - 1)
    def _():
        pl.semaphore_signal(barrier, inc=1, device_id={"seq": rank + 2})

    for step in range(1, n_head):
        pl.semaphore_signal(barrier, inc=1, device_id={"head": lax.rem(col + step, n_head)})

    def head_at(i):
        return lax.rem(x * half + i, heads)

    def columns(i):
        return pl.ds(pl.multiple_of(head_at(i) * DH, DH), DH)

    def rows(n):
        return pl.ds(n * BLOCK, BLOCK)

    row_ids = lax.broadcasted_iota(jnp.int32, (BLOCK, BLOCK), 0)
    col_ids = lax.broadcasted_iota(jnp.int32, (BLOCK, BLOCK), 1)
    loads[0].wait()
    upto = (row_ids <= col_ids).astype(f32)
    shard_total = jnp.zeros((heads, BLOCK), f32)
    for n in range(blocks):
        within = lax.dot_general(
            ld_ref[:, rows(n)],
            upto,
            (((1,), (0,)), ((), ())),
            precision=lax.Precision.HIGHEST,
            preferred_element_type=f32,
        )
        total = jnp.broadcast_to(within[:, BLOCK - 1 : BLOCK], (heads, BLOCK))
        within_ref[n] = within
        total_ref[n] = total
        dec_ref[n] = jnp.exp(total)
        shard_total = shard_total + total
    shard_dec_ref[...] = jnp.exp(shard_total)
    loads[1].wait()
    loads[2].wait()

    def pair_copy(d, i):
        size = DH + 8 if d == 0 else DH
        j = i - half
        return pltpu.make_async_remote_copy(
            src_ref=slab.at[d, i, pl.ds(0, size)],
            dst_ref=pair_in.at[d, j, pl.ds(0, size)],
            send_sem=pair_send.at[d, j],
            recv_sem=pair_recv.at[d, j],
            device_id={"seq": partner},
        )

    def chain_copy(d, j):
        return pltpu.make_async_remote_copy(
            src_ref=chain_out.at[d, j],
            dst_ref=chain_in.at[d, j],
            send_sem=chain_send.at[d, j],
            recv_sem=chain_recv.at[d, j],
            device_id={"seq": rank + 2 - 4 * d},
        )

    def fin_copy(d, j):
        return pltpu.make_async_remote_copy(
            src_ref=pair_out.at[d, j],
            dst_ref=incoming.at[d, half + j],
            send_sem=fin_send.at[d, j],
            recv_sem=fin_recv.at[d, j],
            device_id={"seq": partner},
        )

    def forward_terms(i):
        h = head_at(i)
        at = columns(i)
        state = jnp.zeros((DH, DH), f32)
        for n in range(blocks):
            row = jnp.broadcast_to(within_ref[n, pl.ds(h, 1), :], (BLOCK, BLOCK))
            to_end = jnp.exp(total_ref[n, pl.ds(h, 1), :] - row.T)
            end_ref[i, rows(n)] = to_end
            scaled = (to_end * k_ref[rows(n), at].astype(f32)).astype(bf16)
            term = dot(scaled, v_ref[rows(n), at], 0, 0)
            terms[0, i, n] = term
            state = dec_ref[n, pl.ds(h, 1), :] * state + term
        slab[0, i, pl.ds(0, DH)] = state
        slab[0, i, pl.ds(DH, 8)] = jnp.broadcast_to(shard_dec_ref[pl.ds(h, 1), :], (8, DH))

    def forward_inside(i):
        h = head_at(i)
        at = columns(i)
        for n in range(blocks):
            row = jnp.broadcast_to(within_ref[n, pl.ds(h, 1), :], (BLOCK, BLOCK))
            column = row.T
            mask = jnp.where(
                row_ids >= col_ids, jnp.exp(jnp.minimum(column - row, 0.0)), 0.0
            )
            mask_ref[i, rows(n)] = mask
            grow_ref[i, rows(n)] = jnp.exp(column)
            probs = (dot(q_ref[rows(n), at], k_ref[rows(n), at], 1, 1) * mask).astype(bf16)
            probs_ref[i, rows(n)] = probs
            attn_ref[i, rows(n)] = dot(probs, v_ref[rows(n), at], 1, 0)

    def loop(low, high, body):
        def step(i, carry):
            body(i)
            return carry

        lax.fori_loop(low, high, step, 0)

    def scan(d):
        first = (x == 0) if d == 0 else (x == 1)
        at = z if d == 0 else groups - 1 - z

        def step(j):
            pair_copy(d, half + j).wait_recv()

            @pl.when(at > 0)
            def _():
                chain_copy(d, j).wait_recv()

            @pl.when(at == 0)
            def _():
                chain_in[d, j] = jnp.zeros((DH, DH), f32)

            mine, other = slab[d, j, pl.ds(0, DH)], pair_in[d, j, pl.ds(0, DH)]
            mine_dec, other_dec = slab[0, j, pl.ds(DH, 1)], pair_in[0, j, pl.ds(DH, 1)]
            first_state = jnp.where(first, mine, other)
            last_state = jnp.where(first, other, mine)
            first_dec = jnp.where(first, mine_dec, other_dec)
            last_dec = jnp.where(first, other_dec, mine_dec)
            before = chain_in[d, j]
            between = first_dec * before + first_state
            chain_out[d, j] = last_dec * between + last_state

            @pl.when(at < groups - 1)
            def _():
                chain_copy(d, j).start()

            incoming[d, j] = jnp.where(first, before, between)
            pair_out[d, j] = jnp.where(first, between, before)
            fin_copy(d, j).start()

        loop(0, half, step)

    n_peers = 1 + (z > 0).astype(jnp.int32) + (z < groups - 1).astype(jnp.int32) + n_head - 1
    pl.semaphore_wait(barrier, n_peers)

    def send_terms(i):
        forward_terms(i)
        pair_copy(0, i).start()

    loop(half, heads, send_terms)
    loop(0, half, forward_terms)
    loads[3].wait()
    ahead = (z * heads) // max(groups - 1, 1)
    loop(0, ahead, forward_inside)
    scan(0)
    loop(ahead, heads, forward_inside)
    loads[4].wait()

    acc_ref[...] = jnp.zeros_like(acc_ref)

    def complete(i):
        h = head_at(i)
        at = columns(i)
        state = incoming[0, i]
        for n in range(blocks):
            rounded = state.astype(bf16)
            state_ref[i, n] = rounded
            inter = dot(q_ref[rows(n), at], rounded, 1, 0)
            attn = attn_ref[i, rows(n)] + grow_ref[i, rows(n)] * inter
            attn_ref[i, rows(n)] = attn
            acc_ref[0, rows(n)] += attn * attn
            acc_ref[1, rows(n)] += attn * g_ref[rows(n), at].astype(f32)
            state = dec_ref[n, pl.ds(h, 1), :] * state + terms[0, i, n]

    def complete_foreign(i):
        fin_copy(0, i - half).wait_recv()
        complete(i)

    loop(0, half, complete)
    loop(half, heads, complete_foreign)

    for kind in range(2):
        for n in range(blocks):
            stat_out[pl.ds(kind * blocks + n, 1), :] = jnp.sum(
                acc_ref[kind, rows(n)].T, axis=0, keepdims=True
            )

    def stat_copy(step):
        return pltpu.make_async_remote_copy(
            src_ref=stat_out,
            dst_ref=stat_in.at[step - 1],
            send_sem=stat_send.at[step - 1],
            recv_sem=stat_recv.at[step - 1],
            device_id={"head": lax.rem(col + step, n_head)},
        )

    for step in range(1, n_head):
        stat_copy(step).start()
    stats = stat_out[...]
    for step in range(1, n_head):
        stat_copy(step).wait_recv()
        stats = stats + stat_in[step - 1]
    width = float(HEAD_COUNT * DH)
    inv_rms = lax.rsqrt(stats[:blocks] / width + EPSILON)
    coef = inv_rms * (inv_rms * stats[blocks:] / width)
    for n in range(blocks):
        row_ref[0, rows(n)] = jnp.broadcast_to(inv_rms[n : n + 1], (BLOCK, BLOCK)).T
        row_ref[1, rows(n)] = jnp.broadcast_to(coef[n : n + 1], (BLOCK, BLOCK)).T

    def back_terms(i):
        h = head_at(i)
        at = columns(i)
        state = jnp.zeros((DH, DH), f32)
        for n in reversed(range(blocks)):
            ag = (
                row_ref[0, rows(n)]
                * (g_ref[rows(n), at].astype(f32) - attn_ref[i, rows(n)] * row_ref[1, rows(n)])
            ).astype(bf16)
            ag_ref[i, rows(n)] = ag
            scaled = (grow_ref[i, rows(n)] * q_ref[rows(n), at].astype(f32)).astype(bf16)
            term = dot(scaled, ag, 0, 0)
            terms[1, i, n] = term
            state = dec_ref[n, pl.ds(h, 1), :] * state + term
        slab[1, i, pl.ds(0, DH)] = state

    def send_back_terms(i):
        back_terms(i)
        pair_copy(1, i).start()

    def out_copy(which, i):
        src, dst = ((q_out, qo_hbm), (k_out, ko_hbm), (v_out, vo_hbm))[which]
        return pltpu.make_async_copy(src.at[i], dst.at[:, columns(i)], out_sem.at[which, i])

    def back_inside(i):
        at = columns(i)
        for n in range(blocks):
            ag = ag_ref[i, rows(n)]
            grad = (dot(ag, v_ref[rows(n), at], 1, 1) * mask_ref[i, rows(n)]).astype(bf16)
            query = dot(grad, k_ref[rows(n), at], 1, 0)
            query = query + grow_ref[i, rows(n)] * dot(ag, state_ref[i, n], 1, 1)
            q_out[i, rows(n)] = query.astype(bf16)
            ki_ref[i, rows(n)] = dot(grad, q_ref[rows(n), at], 0, 0)
            vi_ref[i, rows(n)] = dot(probs_ref[i, rows(n)], ag, 0, 0)
        out_copy(0, i).start()

    loop(half, heads, send_back_terms)
    loop(0, half, back_terms)
    back_ahead = ((groups - 1 - z) * heads) // max(groups - 1, 1)
    loop(0, back_ahead, back_inside)
    scan(1)
    loop(back_ahead, heads, back_inside)

    def finish(i):
        h = head_at(i)
        at = columns(i)
        state = incoming[1, i]
        for n in reversed(range(blocks)):
            rounded = state.astype(bf16)
            to_end = end_ref[i, rows(n)]
            key = ki_ref[i, rows(n)] + to_end * dot(v_ref[rows(n), at], rounded, 1, 1)
            value = vi_ref[i, rows(n)] + to_end * dot(k_ref[rows(n), at], rounded, 1, 0)
            k_out[i, rows(n)] = key.astype(bf16)
            v_out[i, rows(n)] = value.astype(bf16)
            state = dec_ref[n, pl.ds(h, 1), :] * state + terms[1, i, n]
        out_copy(1, i).start()
        out_copy(2, i).start()

    def finish_foreign(i):
        fin_copy(1, i - half).wait_recv()
        finish(i)

    loop(0, half, finish)
    loop(half, heads, finish_foreign)

    for step in range(1, n_head):
        stat_copy(step).wait_send()
    for d in range(2):

        def drain(j):
            pair_copy(d, half + j).wait_send()
            fin_copy(d, j).wait_send()

            @pl.when((z < groups - 1) if d == 0 else (z > 0))
            def _():
                chain_copy(d, j).wait_send()

        loop(0, half, drain)

    def drain_out(i):
        for which in range(3):
            out_copy(which, i).wait()

    loop(0, heads, drain_out)


def solution(mesh):
    n_seq, n_head = mesh.shape["seq"], mesh.shape["head"]

    def shards(queries, key_rows, value_rows, out_grad, log_decay):
        tokens, width = queries.shape
        heads = log_decay.shape[0]
        blocks = tokens // BLOCK
        half = heads // 2
        full = (heads, tokens, DH)
        dma = pltpu.SemaphoreType.DMA
        scratch = [
            pltpu.VMEM((tokens, width), bf16),
            pltpu.VMEM((tokens, width), bf16),
            pltpu.VMEM((tokens, width), bf16),
            pltpu.VMEM((tokens, width), bf16),
            pltpu.VMEM((heads, tokens), f32),
            pltpu.VMEM((blocks, heads, BLOCK), f32),
            pltpu.VMEM((blocks, heads, BLOCK), f32),
            pltpu.VMEM((blocks, heads, BLOCK), f32),
            pltpu.VMEM((heads, BLOCK), f32),
            pltpu.VMEM((2, heads, blocks, DH, DH), f32),
            pltpu.VMEM(full, f32),
            pltpu.VMEM(full, f32),
            pltpu.VMEM(full, f32),
            pltpu.VMEM(full, f32),
            pltpu.VMEM(full, bf16),
            pltpu.VMEM(full, bf16),
            pltpu.VMEM((heads, blocks, DH, DH), bf16),
            pltpu.VMEM(full, f32),
            pltpu.VMEM(full, f32),
            pltpu.VMEM((2, heads, DH + 8, DH), f32),
            pltpu.VMEM((2, half, DH + 8, DH), f32),
            pltpu.VMEM((2, half, DH, DH), f32),
            pltpu.VMEM((2, half, DH, DH), f32),
            pltpu.VMEM((2, half, DH, DH), f32),
            pltpu.VMEM((2, heads, DH, DH), f32),
            pltpu.VMEM((2, tokens, DH), f32),
            pltpu.VMEM((2 * blocks, BLOCK), f32),
            pltpu.VMEM((n_head - 1, 2 * blocks, BLOCK), f32),
            pltpu.VMEM((2, tokens, DH), f32),
            pltpu.VMEM(full, bf16),
            pltpu.VMEM(full, bf16),
            pltpu.VMEM(full, bf16),
            dma((5,)),
            dma((2, half)),
            dma((2, half)),
            dma((2, half)),
            dma((2, half)),
            dma((2, half)),
            dma((2, half)),
            dma((n_head - 1,)),
            dma((n_head - 1,)),
            dma((3, heads)),
        ]
        anywhere = pl.BlockSpec(memory_space=pl.ANY)
        return pl.pallas_call(
            functools.partial(kernel, n_seq, n_head),
            out_shape=[jax.ShapeDtypeStruct((tokens, width), bf16)] * 3,
            in_specs=[anywhere] * 5,
            out_specs=[anywhere] * 3,
            scratch_shapes=scratch,
            compiler_params=pltpu.CompilerParams(
                collective_id=0,
                has_side_effects=True,
                vmem_limit_bytes=48 * 1024 * 1024,
            ),
            name="lightning",
        )(queries, key_rows, value_rows, out_grad, log_decay)

    return jax.shard_map(
        shards,
        mesh=mesh,
        in_specs=(
            P("seq", "head"),
            P("seq", "head"),
            P("seq", "head"),
            P("seq", "head"),
            P("head", "seq"),
        ),
        out_specs=(P("seq", "head"), P("seq", "head"), P("seq", "head")),
        check_vma=False,
    )
```

```python
import functools

import jax
import jax.numpy as jnp
from jax import lax
from jax.experimental import pallas as pl
from jax.experimental.pallas import tpu as pltpu
from jax.sharding import PartitionSpec as P

HEAD_COUNT = 32
DH = 128
BLOCK = 128
CUTS = 2
PIECE = DH // CUTS
VMEM_LIMIT = 61 * 1024 * 1024
EPSILON = 1e-06

f32 = jnp.float32
bf16 = jnp.bfloat16


def dot(left, right, left_dim, right_dim):
    return lax.dot_general(
        left, right, (((left_dim,), (right_dim,)), ((), ())), preferred_element_type=f32
    )


def kernel(
    n_seq,
    n_head,
    q_hbm,
    k_hbm,
    v_hbm,
    g_hbm,
    ld_hbm,
    qo_hbm,
    ko_hbm,
    vo_hbm,
    q_ref,
    k_ref,
    v_ref,
    g_ref,
    ld_ref,
    within_ref,
    total_ref,
    dec_ref,
    shard_dec_ref,
    terms,
    mask_ref,
    grow_ref,
    end_ref,
    attn_ref,
    probs_ref,
    ag_ref,
    state_ref,
    ki_ref,
    vi_ref,
    slab,
    pair_in,
    chain_in,
    chain_out,
    pair_out,
    incoming,
    acc_ref,
    stat_out,
    stat_in,
    row_ref,
    q_out,
    k_out,
    v_out,
    load_sem,
    pair_send,
    pair_recv,
    chain_send,
    chain_recv,
    fin_send,
    fin_recv,
    stat_send,
    stat_recv,
    out_sem,
):
    heads = ld_ref.shape[0]
    blocks = ld_ref.shape[1] // BLOCK
    half = heads // 2
    groups = n_seq // 2
    rank = lax.axis_index("seq")
    col = lax.axis_index("head")
    x = lax.rem(rank, 2)
    z = rank // 2
    partner = rank + 1 - 2 * x

    loads = [
        pltpu.make_async_copy(src, dst, load_sem.at[at])
        for at, (src, dst) in enumerate(
            [(ld_hbm, ld_ref), (k_hbm, k_ref), (v_hbm, v_ref), (q_hbm, q_ref), (g_hbm, g_ref)]
        )
    ]
    for load in loads:
        load.start()

    barrier = pltpu.get_barrier_semaphore()
    pl.semaphore_signal(barrier, inc=1, device_id={"seq": partner})

    @pl.when(z > 0)
    def _():
        pl.semaphore_signal(barrier, inc=1, device_id={"seq": rank - 2})

    @pl.when(z < groups - 1)
    def _():
        pl.semaphore_signal(barrier, inc=1, device_id={"seq": rank + 2})

    for step in range(1, n_head):
        pl.semaphore_signal(barrier, inc=1, device_id={"head": lax.rem(col + step, n_head)})

    def head_at(i):
        return lax.rem(x * half + i, heads)

    def columns(i):
        return pl.ds(pl.multiple_of(head_at(i) * DH, DH), DH)

    def rows(n):
        return pl.ds(n * BLOCK, BLOCK)

    row_ids = lax.broadcasted_iota(jnp.int32, (BLOCK, BLOCK), 0)
    col_ids = lax.broadcasted_iota(jnp.int32, (BLOCK, BLOCK), 1)
    loads[0].wait()
    upto = (row_ids <= col_ids).astype(f32)
    shard_total = jnp.zeros((heads, BLOCK), f32)
    for n in range(blocks):
        within = lax.dot_general(
            ld_ref[:, rows(n)],
            upto,
            (((1,), (0,)), ((), ())),
            precision=lax.Precision.HIGHEST,
            preferred_element_type=f32,
        )
        total = jnp.broadcast_to(within[:, BLOCK - 1 : BLOCK], (heads, BLOCK))
        within_ref[n] = within
        total_ref[n] = total
        dec_ref[n] = jnp.exp(total)
        shard_total = shard_total + total
    shard_dec_ref[...] = jnp.exp(shard_total)
    loads[1].wait()
    loads[2].wait()

    def pair_copy(d, i, c):
        size = PIECE + 8 if d == 0 else PIECE
        j = i - half
        return pltpu.make_async_remote_copy(
            src_ref=slab.at[d, i, c, pl.ds(0, size)],
            dst_ref=pair_in.at[d, j, c, pl.ds(0, size)],
            send_sem=pair_send.at[d, j, c],
            recv_sem=pair_recv.at[d, j, c],
            device_id={"seq": partner},
        )

    def chain_copy(d, j, c):
        return pltpu.make_async_remote_copy(
            src_ref=chain_out.at[d, j, c],
            dst_ref=chain_in.at[d, j, c],
            send_sem=chain_send.at[d, j, c],
            recv_sem=chain_recv.at[d, j, c],
            device_id={"seq": rank + 2 - 4 * d},
        )

    def fin_copy(d, j, c):
        return pltpu.make_async_remote_copy(
            src_ref=pair_out.at[d, j, c],
            dst_ref=incoming.at[d, half + j, pl.ds(c * PIECE, PIECE)],
            send_sem=fin_send.at[d, j, c],
            recv_sem=fin_recv.at[d, j, c],
            device_id={"seq": partner},
        )

    def forward_terms(i):
        h = head_at(i)
        at = columns(i)
        state = jnp.zeros((DH, DH), f32)
        for n in range(blocks):
            row = jnp.broadcast_to(within_ref[n, pl.ds(h, 1), :], (BLOCK, BLOCK))
            to_end = jnp.exp(total_ref[n, pl.ds(h, 1), :] - row.T)
            end_ref[i, rows(n)] = to_end
            scaled = (to_end * k_ref[rows(n), at].astype(f32)).astype(bf16)
            term = dot(scaled, v_ref[rows(n), at], 0, 0)
            terms[0, i, n] = term
            state = dec_ref[n, pl.ds(h, 1), :] * state + term
        for c in range(CUTS):
            slab[0, i, c, pl.ds(0, PIECE)] = state[c * PIECE : (c + 1) * PIECE]
            slab[0, i, c, pl.ds(PIECE, 8)] = jnp.broadcast_to(
                shard_dec_ref[pl.ds(h, 1), :], (8, DH)
            )

    def forward_inside(i):
        h = head_at(i)
        at = columns(i)
        for n in range(blocks):
            row = jnp.broadcast_to(within_ref[n, pl.ds(h, 1), :], (BLOCK, BLOCK))
            column = row.T
            mask = jnp.where(
                row_ids >= col_ids, jnp.exp(jnp.minimum(column - row, 0.0)), 0.0
            )
            mask_ref[i, rows(n)] = mask
            grow_ref[i, rows(n)] = jnp.exp(column)
            probs = (dot(q_ref[rows(n), at], k_ref[rows(n), at], 1, 1) * mask).astype(bf16)
            probs_ref[i, rows(n)] = probs
            attn_ref[i, rows(n)] = dot(probs, v_ref[rows(n), at], 1, 0)

    def loop(low, high, body):
        def step(i, carry):
            body(i)
            return carry

        lax.fori_loop(low, high, step, 0)

    def scan(d, unit):
        first = (x == 0) if d == 0 else (x == 1)
        at = z if d == 0 else groups - 1 - z

        def step(j):
            for c in range(CUTS):
                pair_copy(d, half + j, c).wait_recv()

                @pl.when(at > 0)
                def _():
                    chain_copy(d, j, c).wait_recv()

                @pl.when(at == 0)
                def _():
                    chain_in[d, j, c] = jnp.zeros((PIECE, DH), f32)

                mine, other = slab[d, j, c, pl.ds(0, PIECE)], pair_in[d, j, c, pl.ds(0, PIECE)]
                mine_dec = slab[0, j, c, pl.ds(PIECE, 1)]
                other_dec = pair_in[0, j, c, pl.ds(PIECE, 1)]
                first_state = jnp.where(first, mine, other)
                last_state = jnp.where(first, other, mine)
                first_dec = jnp.where(first, mine_dec, other_dec)
                last_dec = jnp.where(first, other_dec, mine_dec)
                before = chain_in[d, j, c]
                between = first_dec * before + first_state
                chain_out[d, j, c] = last_dec * between + last_state

                @pl.when(at < groups - 1)
                def _():
                    chain_copy(d, j, c).start()

                incoming[d, j, pl.ds(c * PIECE, PIECE)] = jnp.where(first, before, between)
                pair_out[d, j, c] = jnp.where(first, between, before)
                fin_copy(d, j, c).start()
            unit(j)

        loop(0, half, step)

    n_peers = 1 + (z > 0).astype(jnp.int32) + (z < groups - 1).astype(jnp.int32) + n_head - 1
    pl.semaphore_wait(barrier, n_peers)

    def send_terms(i):
        forward_terms(i)
        for c in range(CUTS):
            pair_copy(0, i, c).start()

    loop(half, heads, send_terms)
    loop(0, half, forward_terms)
    loads[3].wait()
    acc_ref[...] = jnp.zeros_like(acc_ref)

    def complete(i):
        h = head_at(i)
        at = columns(i)
        state = incoming[0, i]
        for n in range(blocks):
            rounded = state.astype(bf16)
            state_ref[i, n] = rounded
            inter = dot(q_ref[rows(n), at], rounded, 1, 0)
            attn = attn_ref[i, rows(n)] + grow_ref[i, rows(n)] * inter
            attn_ref[i, rows(n)] = attn
            acc_ref[0, rows(n)] += attn * attn
            acc_ref[1, rows(n)] += attn * g_ref[rows(n), at].astype(f32)
            state = dec_ref[n, pl.ds(h, 1), :] * state + terms[0, i, n]

    def complete_foreign(i):
        for c in range(CUTS):
            fin_copy(0, i - half, c).wait_recv()
        complete(i)

    def units(ahead, inside, after):
        def unit(j):
            @pl.when(ahead + j < heads)
            def _():
                inside(ahead + j)

            @pl.when(ahead + j >= heads)
            def _():
                after(ahead + j - heads)

        return unit

    def run(d, at, inside, after, after_foreign):
        ahead = (at * heads) // max(groups - 1, 1)
        loop(0, ahead, inside)
        scan(d, units(ahead, inside, after))
        loop(ahead + half, heads, inside)
        loop(jnp.maximum(ahead + half - heads, 0), half, after)
        loop(half, heads, after_foreign)

    loads[4].wait()
    run(0, z, forward_inside, complete, complete_foreign)

    for kind in range(2):
        for n in range(blocks):
            stat_out[pl.ds(kind * blocks + n, 1), :] = jnp.sum(
                acc_ref[kind, rows(n)].T, axis=0, keepdims=True
            )

    def stat_copy(step):
        return pltpu.make_async_remote_copy(
            src_ref=stat_out,
            dst_ref=stat_in.at[step - 1],
            send_sem=stat_send.at[step - 1],
            recv_sem=stat_recv.at[step - 1],
            device_id={"head": lax.rem(col + step, n_head)},
        )

    for step in range(1, n_head):
        stat_copy(step).start()
    stats = stat_out[...]
    for step in range(1, n_head):
        stat_copy(step).wait_recv()
        stats = stats + stat_in[step - 1]
    width = float(HEAD_COUNT * DH)
    inv_rms = lax.rsqrt(stats[:blocks] / width + EPSILON)
    coef = inv_rms * (inv_rms * stats[blocks:] / width)
    for n in range(blocks):
        row_ref[0, rows(n)] = jnp.broadcast_to(inv_rms[n : n + 1], (BLOCK, BLOCK)).T
        row_ref[1, rows(n)] = jnp.broadcast_to(coef[n : n + 1], (BLOCK, BLOCK)).T

    def back_terms(i):
        h = head_at(i)
        at = columns(i)
        state = jnp.zeros((DH, DH), f32)
        for n in reversed(range(blocks)):
            ag = (
                row_ref[0, rows(n)]
                * (g_ref[rows(n), at].astype(f32) - attn_ref[i, rows(n)] * row_ref[1, rows(n)])
            ).astype(bf16)
            ag_ref[i, rows(n)] = ag
            scaled = (grow_ref[i, rows(n)] * q_ref[rows(n), at].astype(f32)).astype(bf16)
            term = dot(scaled, ag, 0, 0)
            terms[1, i, n] = term
            state = dec_ref[n, pl.ds(h, 1), :] * state + term
        for c in range(CUTS):
            slab[1, i, c, pl.ds(0, PIECE)] = state[c * PIECE : (c + 1) * PIECE]

    def send_back_terms(i):
        back_terms(i)
        for c in range(CUTS):
            pair_copy(1, i, c).start()

    def out_copy(which, i):
        src, dst = ((q_out, qo_hbm), (k_out, ko_hbm), (v_out, vo_hbm))[which]
        return pltpu.make_async_copy(src.at[i], dst.at[:, columns(i)], out_sem.at[which, i])

    def back_inside(i):
        at = columns(i)
        for n in range(blocks):
            ag = ag_ref[i, rows(n)]
            grad = (dot(ag, v_ref[rows(n), at], 1, 1) * mask_ref[i, rows(n)]).astype(bf16)
            query = dot(grad, k_ref[rows(n), at], 1, 0)
            query = query + grow_ref[i, rows(n)] * dot(ag, state_ref[i, n], 1, 1)
            q_out[i, rows(n)] = query.astype(bf16)
            ki_ref[i, rows(n)] = dot(grad, q_ref[rows(n), at], 0, 0)
            vi_ref[i, rows(n)] = dot(probs_ref[i, rows(n)], ag, 0, 0)
        out_copy(0, i).start()

    loop(half, heads, send_back_terms)
    loop(0, half, back_terms)

    def finish(i):
        h = head_at(i)
        at = columns(i)
        state = incoming[1, i]
        for n in reversed(range(blocks)):
            rounded = state.astype(bf16)
            to_end = end_ref[i, rows(n)]
            key = ki_ref[i, rows(n)] + to_end * dot(v_ref[rows(n), at], rounded, 1, 1)
            value = vi_ref[i, rows(n)] + to_end * dot(k_ref[rows(n), at], rounded, 1, 0)
            k_out[i, rows(n)] = key.astype(bf16)
            v_out[i, rows(n)] = value.astype(bf16)
            state = dec_ref[n, pl.ds(h, 1), :] * state + terms[1, i, n]
        out_copy(1, i).start()
        out_copy(2, i).start()

    def finish_foreign(i):
        for c in range(CUTS):
            fin_copy(1, i - half, c).wait_recv()
        finish(i)

    run(1, groups - 1 - z, back_inside, finish, finish_foreign)

    for step in range(1, n_head):
        stat_copy(step).wait_send()
    for d in range(2):

        def drain(j):
            for c in range(CUTS):
                pair_copy(d, half + j, c).wait_send()
                fin_copy(d, j, c).wait_send()

                @pl.when((z < groups - 1) if d == 0 else (z > 0))
                def _():
                    chain_copy(d, j, c).wait_send()

        loop(0, half, drain)

    def drain_out(i):
        for which in range(3):
            out_copy(which, i).wait()

    loop(0, heads, drain_out)


def write_out(q_in, k_in, v_in, q_hbm, k_hbm, v_hbm, sem):
    copies = [
        pltpu.make_async_copy(
            src.at[pl.ds(n * BLOCK, BLOCK)], dst.at[pl.ds(n * BLOCK, BLOCK)], sem.at[at, n]
        )
        for at, (src, dst) in enumerate([(q_in, q_hbm), (k_in, k_hbm), (v_in, v_hbm)])
        for n in range(q_in.shape[0] // BLOCK)
    ]
    for copy in copies:
        copy.start()
    for copy in copies:
        copy.wait()


def solution(mesh):
    n_seq, n_head = mesh.shape["seq"], mesh.shape["head"]

    def shards(queries, key_rows, value_rows, out_grad, log_decay):
        tokens, width = queries.shape
        heads = log_decay.shape[0]
        blocks = tokens // BLOCK
        half = heads // 2
        full = (heads, tokens, DH)
        dma = pltpu.SemaphoreType.DMA
        scratch = [
            pltpu.VMEM((tokens, width), bf16),
            pltpu.VMEM((tokens, width), bf16),
            pltpu.VMEM((tokens, width), bf16),
            pltpu.VMEM((tokens, width), bf16),
            pltpu.VMEM((heads, tokens), f32),
            pltpu.VMEM((blocks, heads, BLOCK), f32),
            pltpu.VMEM((blocks, heads, BLOCK), f32),
            pltpu.VMEM((blocks, heads, BLOCK), f32),
            pltpu.VMEM((heads, BLOCK), f32),
            pltpu.VMEM((2, heads, blocks, DH, DH), f32),
            pltpu.VMEM(full, f32),
            pltpu.VMEM(full, f32),
            pltpu.VMEM(full, f32),
            pltpu.VMEM(full, f32),
            pltpu.VMEM(full, bf16),
            pltpu.VMEM(full, bf16),
            pltpu.VMEM((heads, blocks, DH, DH), bf16),
            pltpu.VMEM(full, f32),
            pltpu.VMEM(full, f32),
            pltpu.VMEM((2, heads, CUTS, PIECE + 8, DH), f32),
            pltpu.VMEM((2, half, CUTS, PIECE + 8, DH), f32),
            pltpu.VMEM((2, half, CUTS, PIECE, DH), f32),
            pltpu.VMEM((2, half, CUTS, PIECE, DH), f32),
            pltpu.VMEM((2, half, CUTS, PIECE, DH), f32),
            pltpu.VMEM((2, heads, DH, DH), f32),
            pltpu.VMEM((2, tokens, DH), f32),
            pltpu.VMEM((2 * blocks, BLOCK), f32),
            pltpu.VMEM((n_head - 1, 2 * blocks, BLOCK), f32),
            pltpu.VMEM((2, tokens, DH), f32),
            pltpu.VMEM(full, bf16),
            pltpu.VMEM(full, bf16),
            pltpu.VMEM(full, bf16),
            dma((5,)),
            dma((2, half, CUTS)),
            dma((2, half, CUTS)),
            dma((2, half, CUTS)),
            dma((2, half, CUTS)),
            dma((2, half, CUTS)),
            dma((2, half, CUTS)),
            dma((n_head - 1,)),
            dma((n_head - 1,)),
            dma((3, heads)),
        ]
        anywhere = pl.BlockSpec(memory_space=pl.ANY)
        in_hbm = pl.BlockSpec(memory_space=pltpu.HBM)
        results = pl.pallas_call(
            functools.partial(kernel, n_seq, n_head),
            out_shape=[jax.ShapeDtypeStruct((tokens, width), bf16)] * 3,
            in_specs=[in_hbm] * 5,
            out_specs=[anywhere] * 3,
            scratch_shapes=scratch,
            compiler_params=pltpu.CompilerParams(
                collective_id=0,
                has_side_effects=True,
                vmem_limit_bytes=VMEM_LIMIT,
            ),
            name="lightning",
        )(queries, key_rows, value_rows, out_grad, log_decay)
        return pl.pallas_call(
            write_out,
            out_shape=[jax.ShapeDtypeStruct((tokens, width), bf16)] * 3,
            in_specs=[anywhere] * 3,
            out_specs=[in_hbm] * 3,
            scratch_shapes=[dma((3, blocks))],
            compiler_params=pltpu.CompilerParams(vmem_limit_bytes=VMEM_LIMIT),
            name="write_out",
        )(*results)

    return jax.shard_map(
        shards,
        mesh=mesh,
        in_specs=(
            P("seq", "head"),
            P("seq", "head"),
            P("seq", "head"),
            P("seq", "head"),
            P("head", "seq"),
        ),
        out_specs=(P("seq", "head"), P("seq", "head"), P("seq", "head")),
        check_vma=False,
    )
```

```python
import functools

import jax
import jax.numpy as jnp
from jax import lax
from jax.experimental import pallas as pl
from jax.experimental.pallas import tpu as pltpu
from jax.sharding import PartitionSpec as P

HEAD_COUNT = 32
DH = 128
BLOCK = 128
CUTS = 2
PIECE = DH // CUTS
VMEM_LIMIT = 61 * 1024 * 1024
EPSILON = 1e-06

f32 = jnp.float32
bf16 = jnp.bfloat16


def dot(left, right, left_dim, right_dim):
    return lax.dot_general(
        left, right, (((left_dim,), (right_dim,)), ((), ())), preferred_element_type=f32
    )


def kernel(
    n_seq,
    n_head,
    q_hbm,
    k_hbm,
    v_hbm,
    g_hbm,
    ld_hbm,
    qo_hbm,
    ko_hbm,
    vo_hbm,
    q_ref,
    k_ref,
    v_ref,
    g_ref,
    ld_ref,
    within_ref,
    column_ref,
    total_ref,
    dec_ref,
    shard_dec_ref,
    terms,
    mask_ref,
    grow_ref,
    end_ref,
    attn_ref,
    probs_ref,
    ag_ref,
    state_ref,
    ki_ref,
    vi_ref,
    slab,
    pair_in,
    chain_in,
    chain_out,
    pair_out,
    incoming,
    acc_ref,
    stat_out,
    stat_in,
    row_ref,
    q_out,
    k_out,
    v_out,
    load_sem,
    pair_send,
    pair_recv,
    chain_send,
    chain_recv,
    fin_send,
    fin_recv,
    stat_send,
    stat_recv,
    out_sem,
):
    heads = ld_ref.shape[0]
    blocks = ld_ref.shape[1] // BLOCK
    half = heads // 2
    groups = n_seq // 2
    rank = lax.axis_index("seq")
    col = lax.axis_index("head")
    x = lax.rem(rank, 2)
    z = rank // 2
    partner = rank + 1 - 2 * x

    half_width = half * DH
    near = pl.ds(pl.multiple_of(x * half_width, DH), half_width)
    far = pl.ds(pl.multiple_of((1 - x) * half_width, DH), half_width)
    loads = [
        pltpu.make_async_copy(src, dst, load_sem.at[at])
        for at, (src, dst) in enumerate(
            [
                (ld_hbm, ld_ref),
                (k_hbm.at[:, far], k_ref.at[:, far]),
                (v_hbm.at[:, far], v_ref.at[:, far]),
                (k_hbm.at[:, near], k_ref.at[:, near]),
                (v_hbm.at[:, near], v_ref.at[:, near]),
                (q_hbm, q_ref),
                (g_hbm, g_ref),
            ]
        )
    ]
    for load in loads:
        load.start()

    barrier = pltpu.get_barrier_semaphore()
    pl.semaphore_signal(barrier, inc=1, device_id={"seq": partner})

    @pl.when(z > 0)
    def _():
        pl.semaphore_signal(barrier, inc=1, device_id={"seq": rank - 2})

    @pl.when(z < groups - 1)
    def _():
        pl.semaphore_signal(barrier, inc=1, device_id={"seq": rank + 2})

    for step in range(1, n_head):
        pl.semaphore_signal(barrier, inc=1, device_id={"head": lax.rem(col + step, n_head)})

    def head_at(i):
        return lax.rem(x * half + i, heads)

    def columns(i):
        return pl.ds(pl.multiple_of(head_at(i) * DH, DH), DH)

    def rows(n):
        return pl.ds(n * BLOCK, BLOCK)

    row_ids = lax.broadcasted_iota(jnp.int32, (BLOCK, BLOCK), 0)
    col_ids = lax.broadcasted_iota(jnp.int32, (BLOCK, BLOCK), 1)
    loads[0].wait()
    upto = (row_ids <= col_ids).astype(f32)
    since = (row_ids >= col_ids).astype(f32)
    shard_total = jnp.zeros((heads, BLOCK), f32)
    for n in range(blocks):
        within = lax.dot_general(
            ld_ref[:, rows(n)],
            upto,
            (((1,), (0,)), ((), ())),
            precision=lax.Precision.HIGHEST,
            preferred_element_type=f32,
        )
        total = jnp.broadcast_to(within[:, BLOCK - 1 : BLOCK], (heads, BLOCK))
        by_column = lax.dot_general(
            since,
            ld_ref[:, rows(n)],
            (((1,), (1,)), ((), ())),
            precision=lax.Precision.HIGHEST,
            preferred_element_type=f32,
        )
        for h in range(heads):
            column_ref[h, rows(n)] = jnp.broadcast_to(by_column[:, h : h + 1], (BLOCK, BLOCK))
        within_ref[n] = within
        total_ref[n] = total
        dec_ref[n] = jnp.exp(total)
        shard_total = shard_total + total
    shard_dec_ref[...] = jnp.exp(shard_total)
    loads[1].wait()
    loads[2].wait()

    def pair_copy(d, i, c):
        size = PIECE + 8 if d == 0 else PIECE
        j = i - half
        return pltpu.make_async_remote_copy(
            src_ref=slab.at[d, i, c, pl.ds(0, size)],
            dst_ref=pair_in.at[d, j, c, pl.ds(0, size)],
            send_sem=pair_send.at[d, j, c],
            recv_sem=pair_recv.at[d, j, c],
            device_id={"seq": partner},
        )

    def chain_copy(d, j, c):
        return pltpu.make_async_remote_copy(
            src_ref=chain_out.at[d, j, c],
            dst_ref=chain_in.at[d, j, c],
            send_sem=chain_send.at[d, j, c],
            recv_sem=chain_recv.at[d, j, c],
            device_id={"seq": rank + 2 - 4 * d},
        )

    def fin_copy(d, j, c):
        return pltpu.make_async_remote_copy(
            src_ref=pair_out.at[d, j, c],
            dst_ref=incoming.at[d, half + j, pl.ds(c * PIECE, PIECE)],
            send_sem=fin_send.at[d, j, c],
            recv_sem=fin_recv.at[d, j, c],
            device_id={"seq": partner},
        )

    def forward_terms(i):
        h = head_at(i)
        at = columns(i)
        state = jnp.zeros((DH, DH), f32)
        for n in range(blocks):
            to_end = jnp.exp(total_ref[n, pl.ds(h, 1), :] - column_ref[h, rows(n)])
            end_ref[i, rows(n)] = to_end
            scaled = (to_end * k_ref[rows(n), at].astype(f32)).astype(bf16)
            term = dot(scaled, v_ref[rows(n), at], 0, 0)
            terms[0, i, n] = term
            state = dec_ref[n, pl.ds(h, 1), :] * state + term
        for c in range(CUTS):
            slab[0, i, c, pl.ds(0, PIECE)] = state[c * PIECE : (c + 1) * PIECE]
            slab[0, i, c, pl.ds(PIECE, 8)] = jnp.broadcast_to(
                shard_dec_ref[pl.ds(h, 1), :], (8, DH)
            )

    def forward_inside(i):
        h = head_at(i)
        at = columns(i)
        for n in range(blocks):
            row = within_ref[n, pl.ds(h, 1), :]
            column = column_ref[h, rows(n)]
            mask = jnp.where(
                row_ids >= col_ids, jnp.exp(jnp.minimum(column - row, 0.0)), 0.0
            )
            mask_ref[i, rows(n)] = mask
            grow_ref[i, rows(n)] = jnp.exp(column)
            probs = (dot(q_ref[rows(n), at], k_ref[rows(n), at], 1, 1) * mask).astype(bf16)
            probs_ref[i, rows(n)] = probs
            attn_ref[i, rows(n)] = dot(probs, v_ref[rows(n), at], 1, 0)

    def loop(low, high, body):
        def step(i, carry):
            body(i)
            return carry

        lax.fori_loop(low, high, step, 0)

    def scan(d, unit):
        first = (x == 0) if d == 0 else (x == 1)
        at = z if d == 0 else groups - 1 - z

        def step(j):
            for c in range(CUTS):
                pair_copy(d, half + j, c).wait_recv()

                @pl.when(at > 0)
                def _():
                    chain_copy(d, j, c).wait_recv()

                @pl.when(at == 0)
                def _():
                    chain_in[d, j, c] = jnp.zeros((PIECE, DH), f32)

                mine, other = slab[d, j, c, pl.ds(0, PIECE)], pair_in[d, j, c, pl.ds(0, PIECE)]
                mine_dec = slab[0, j, c, pl.ds(PIECE, 1)]
                other_dec = pair_in[0, j, c, pl.ds(PIECE, 1)]
                first_state = jnp.where(first, mine, other)
                last_state = jnp.where(first, other, mine)
                first_dec = jnp.where(first, mine_dec, other_dec)
                last_dec = jnp.where(first, other_dec, mine_dec)
                before = chain_in[d, j, c]
                between = first_dec * before + first_state
                chain_out[d, j, c] = last_dec * between + last_state

                @pl.when(at < groups - 1)
                def _():
                    chain_copy(d, j, c).start()

                incoming[d, j, pl.ds(c * PIECE, PIECE)] = jnp.where(first, before, between)
                pair_out[d, j, c] = jnp.where(first, between, before)
                fin_copy(d, j, c).start()
            unit(j)

        loop(0, half, step)

    n_peers = 1 + (z > 0).astype(jnp.int32) + (z < groups - 1).astype(jnp.int32) + n_head - 1
    pl.semaphore_wait(barrier, n_peers)

    def send_terms(i):
        forward_terms(i)
        for c in range(CUTS):
            pair_copy(0, i, c).start()

    loop(half, heads, send_terms)
    loads[3].wait()
    loads[4].wait()
    loop(0, half, forward_terms)
    loads[5].wait()
    acc_ref[...] = jnp.zeros_like(acc_ref)

    def complete(i):
        h = head_at(i)
        at = columns(i)
        state = incoming[0, i]
        for n in range(blocks):
            rounded = state.astype(bf16)
            state_ref[i, n] = rounded
            inter = dot(q_ref[rows(n), at], rounded, 1, 0)
            attn = attn_ref[i, rows(n)] + grow_ref[i, rows(n)] * inter
            attn_ref[i, rows(n)] = attn
            acc_ref[0, rows(n)] += attn * attn
            acc_ref[1, rows(n)] += attn * g_ref[rows(n), at].astype(f32)
            state = dec_ref[n, pl.ds(h, 1), :] * state + terms[0, i, n]

    def complete_foreign(i):
        for c in range(CUTS):
            fin_copy(0, i - half, c).wait_recv()
        complete(i)

    def units(ahead, inside, after):
        def unit(j):
            @pl.when(ahead + j < heads)
            def _():
                inside(ahead + j)

            @pl.when(ahead + j >= heads)
            def _():
                after(ahead + j - heads)

        return unit

    def run(d, at, inside, after, after_foreign):
        ahead = (at * heads) // max(groups - 1, 1)
        loop(0, ahead, inside)
        scan(d, units(ahead, inside, after))
        loop(ahead + half, heads, inside)
        loop(jnp.maximum(ahead + half - heads, 0), half, after)
        loop(half, heads, after_foreign)

    loads[6].wait()
    run(0, z, forward_inside, complete, complete_foreign)

    sums = [
        jnp.sum(acc_ref[kind, rows(n)], axis=1, keepdims=True)
        for kind in range(2)
        for n in range(blocks)
    ]
    stat_out[...] = jnp.concatenate(sums, axis=1).T

    def stat_copy(step):
        return pltpu.make_async_remote_copy(
            src_ref=stat_out,
            dst_ref=stat_in.at[step - 1],
            send_sem=stat_send.at[step - 1],
            recv_sem=stat_recv.at[step - 1],
            device_id={"head": lax.rem(col + step, n_head)},
        )

    for step in range(1, n_head):
        stat_copy(step).start()
    stats = stat_out[...]
    for step in range(1, n_head):
        stat_copy(step).wait_recv()
        stats = stats + stat_in[step - 1]
    width = float(HEAD_COUNT * DH)
    inv_rms = lax.rsqrt(stats[:blocks] / width + EPSILON)
    coef = inv_rms * (inv_rms * stats[blocks:] / width)
    scales = jnp.concatenate([inv_rms, coef], axis=0).T
    for kind in range(2):
        for n in range(blocks):
            at = kind * blocks + n
            row_ref[kind, rows(n)] = jnp.broadcast_to(scales[:, at : at + 1], (BLOCK, BLOCK))

    def back_terms(i):
        h = head_at(i)
        at = columns(i)
        state = jnp.zeros((DH, DH), f32)
        for n in reversed(range(blocks)):
            ag = (
                row_ref[0, rows(n)]
                * (g_ref[rows(n), at].astype(f32) - attn_ref[i, rows(n)] * row_ref[1, rows(n)])
            ).astype(bf16)
            ag_ref[i, rows(n)] = ag
            scaled = (grow_ref[i, rows(n)] * q_ref[rows(n), at].astype(f32)).astype(bf16)
            term = dot(scaled, ag, 0, 0)
            terms[1, i, n] = term
            state = dec_ref[n, pl.ds(h, 1), :] * state + term
        for c in range(CUTS):
            slab[1, i, c, pl.ds(0, PIECE)] = state[c * PIECE : (c + 1) * PIECE]

    def send_back_terms(i):
        back_terms(i)
        for c in range(CUTS):
            pair_copy(1, i, c).start()

    def out_copy(which, i):
        src, dst = ((q_out, qo_hbm), (k_out, ko_hbm), (v_out, vo_hbm))[which]
        return pltpu.make_async_copy(src.at[i], dst.at[:, columns(i)], out_sem.at[which, i])

    def back_inside(i):
        at = columns(i)
        for n in range(blocks):
            ag = ag_ref[i, rows(n)]
            grad = (dot(ag, v_ref[rows(n), at], 1, 1) * mask_ref[i, rows(n)]).astype(bf16)
            query = dot(grad, k_ref[rows(n), at], 1, 0)
            query = query + grow_ref[i, rows(n)] * dot(ag, state_ref[i, n], 1, 1)
            q_out[i, rows(n)] = query.astype(bf16)
            ki_ref[i, rows(n)] = dot(grad, q_ref[rows(n), at], 0, 0)
            vi_ref[i, rows(n)] = dot(probs_ref[i, rows(n)], ag, 0, 0)
        out_copy(0, i).start()

    loop(half, heads, send_back_terms)
    loop(0, half, back_terms)

    def finish(i):
        h = head_at(i)
        at = columns(i)
        state = incoming[1, i]
        for n in reversed(range(blocks)):
            rounded = state.astype(bf16)
            to_end = end_ref[i, rows(n)]
            key = ki_ref[i, rows(n)] + to_end * dot(v_ref[rows(n), at], rounded, 1, 1)
            value = vi_ref[i, rows(n)] + to_end * dot(k_ref[rows(n), at], rounded, 1, 0)
            k_out[i, rows(n)] = key.astype(bf16)
            v_out[i, rows(n)] = value.astype(bf16)
            state = dec_ref[n, pl.ds(h, 1), :] * state + terms[1, i, n]
        out_copy(1, i).start()
        out_copy(2, i).start()

    def finish_foreign(i):
        for c in range(CUTS):
            fin_copy(1, i - half, c).wait_recv()
        finish(i)

    run(1, groups - 1 - z, back_inside, finish, finish_foreign)

    for step in range(1, n_head):
        stat_copy(step).wait_send()
    for d in range(2):

        def drain(j):
            for c in range(CUTS):
                pair_copy(d, half + j, c).wait_send()
                fin_copy(d, j, c).wait_send()

                @pl.when((z < groups - 1) if d == 0 else (z > 0))
                def _():
                    chain_copy(d, j, c).wait_send()

        loop(0, half, drain)

    def drain_out(i):
        for which in range(3):
            out_copy(which, i).wait()

    loop(0, heads, drain_out)


def write_out(q_in, k_in, v_in, q_hbm, k_hbm, v_hbm, stage, in_sem, out_sem):
    reads, writes = [], []
    for at, (src, dst) in enumerate([(q_in, q_hbm), (k_in, k_hbm), (v_in, v_hbm)]):
        for n in range(src.shape[0] // BLOCK):
            part = pl.ds(n * BLOCK, BLOCK)
            held = stage.at[at, part]
            reads.append(pltpu.make_async_copy(src.at[part], held, in_sem.at[at, n]))
            writes.append(pltpu.make_async_copy(held, dst.at[part], out_sem.at[at, n]))
    for read in reads:
        read.start()
    for read, write in zip(reads, writes):
        read.wait()
        write.start()
    for write in writes:
        write.wait()


def solution(mesh):
    n_seq, n_head = mesh.shape["seq"], mesh.shape["head"]

    def shards(queries, key_rows, value_rows, out_grad, log_decay):
        tokens, width = queries.shape
        heads = log_decay.shape[0]
        blocks = tokens // BLOCK
        half = heads // 2
        full = (heads, tokens, DH)
        dma = pltpu.SemaphoreType.DMA
        scratch = [
            pltpu.VMEM((tokens, width), bf16),
            pltpu.VMEM((tokens, width), bf16),
            pltpu.VMEM((tokens, width), bf16),
            pltpu.VMEM((tokens, width), bf16),
            pltpu.VMEM((heads, tokens), f32),
            pltpu.VMEM((blocks, heads, BLOCK), f32),
            pltpu.VMEM(full, f32),
            pltpu.VMEM((blocks, heads, BLOCK), f32),
            pltpu.VMEM((blocks, heads, BLOCK), f32),
            pltpu.VMEM((heads, BLOCK), f32),
            pltpu.VMEM((2, heads, blocks, DH, DH), f32),
            pltpu.VMEM(full, f32),
            pltpu.VMEM(full, f32),
            pltpu.VMEM(full, f32),
            pltpu.VMEM(full, f32),
            pltpu.VMEM(full, bf16),
            pltpu.VMEM(full, bf16),
            pltpu.VMEM((heads, blocks, DH, DH), bf16),
            pltpu.VMEM(full, f32),
            pltpu.VMEM(full, f32),
            pltpu.VMEM((2, heads, CUTS, PIECE + 8, DH), f32),
            pltpu.VMEM((2, half, CUTS, PIECE + 8, DH), f32),
            pltpu.VMEM((2, half, CUTS, PIECE, DH), f32),
            pltpu.VMEM((2, half, CUTS, PIECE, DH), f32),
            pltpu.VMEM((2, half, CUTS, PIECE, DH), f32),
            pltpu.VMEM((2, heads, DH, DH), f32),
            pltpu.VMEM((2, tokens, DH), f32),
            pltpu.VMEM((2 * blocks, BLOCK), f32),
            pltpu.VMEM((n_head - 1, 2 * blocks, BLOCK), f32),
            pltpu.VMEM((2, tokens, DH), f32),
            pltpu.VMEM(full, bf16),
            pltpu.VMEM(full, bf16),
            pltpu.VMEM(full, bf16),
            dma((7,)),
            dma((2, half, CUTS)),
            dma((2, half, CUTS)),
            dma((2, half, CUTS)),
            dma((2, half, CUTS)),
            dma((2, half, CUTS)),
            dma((2, half, CUTS)),
            dma((n_head - 1,)),
            dma((n_head - 1,)),
            dma((3, heads)),
        ]
        anywhere = pl.BlockSpec(memory_space=pl.ANY)
        in_hbm = pl.BlockSpec(memory_space=pltpu.HBM)
        results = pl.pallas_call(
            functools.partial(kernel, n_seq, n_head),
            out_shape=[jax.ShapeDtypeStruct((tokens, width), bf16)] * 3,
            in_specs=[in_hbm] * 5,
            out_specs=[anywhere] * 3,
            scratch_shapes=scratch,
            compiler_params=pltpu.CompilerParams(
                collective_id=0,
                has_side_effects=True,
                vmem_limit_bytes=VMEM_LIMIT,
            ),
            name="lightning",
        )(queries, key_rows, value_rows, out_grad, log_decay)
        return pl.pallas_call(
            write_out,
            out_shape=[jax.ShapeDtypeStruct((tokens, width), bf16)] * 3,
            in_specs=[anywhere] * 3,
            out_specs=[in_hbm] * 3,
            scratch_shapes=[
                pltpu.VMEM((3, tokens, width), bf16),
                dma((3, blocks)),
                dma((3, blocks)),
            ],
            compiler_params=pltpu.CompilerParams(vmem_limit_bytes=VMEM_LIMIT),
            name="write_out",
        )(*results)

    return jax.shard_map(
        shards,
        mesh=mesh,
        in_specs=(
            P("seq", "head"),
            P("seq", "head"),
            P("seq", "head"),
            P("seq", "head"),
            P("head", "seq"),
        ),
        out_specs=(P("seq", "head"), P("seq", "head"), P("seq", "head")),
        check_vma=False,
    )
```

```python
import functools

import jax
import jax.numpy as jnp
from jax import lax
from jax.experimental import pallas as pl
from jax.experimental.pallas import tpu as pltpu
from jax.sharding import PartitionSpec as P

HEAD_COUNT = 32
DH = 128
BLOCK = 128
CUTS = 2
PIECE = DH // CUTS
VMEM_LIMIT = 61 * 1024 * 1024
EPSILON = 1e-06

f32 = jnp.float32
bf16 = jnp.bfloat16


def dot(left, right, left_dim, right_dim):
    return lax.dot_general(
        left, right, (((left_dim,), (right_dim,)), ((), ())), preferred_element_type=f32
    )


def kernel(
    n_seq,
    n_head,
    q_hbm,
    k_hbm,
    v_hbm,
    g_hbm,
    ld_hbm,
    qo_hbm,
    ko_hbm,
    vo_hbm,
    q_ref,
    k_ref,
    v_ref,
    g_ref,
    ld_ref,
    within_ref,
    column_ref,
    total_ref,
    dec_ref,
    shard_dec_ref,
    terms,
    mask_ref,
    grow_ref,
    end_ref,
    attn_ref,
    probs_ref,
    ag_ref,
    state_ref,
    ki_ref,
    vi_ref,
    slab,
    pair_in,
    chain_in,
    chain_out,
    pair_out,
    incoming,
    acc_ref,
    stat_out,
    stat_in,
    row_ref,
    q_out,
    k_out,
    v_out,
    load_sem,
    pair_send,
    pair_recv,
    chain_send,
    chain_recv,
    fin_send,
    fin_recv,
    stat_send,
    stat_recv,
    out_sem,
):
    heads = ld_ref.shape[0]
    blocks = ld_ref.shape[1] // BLOCK
    half = heads // 2
    groups = n_seq // 2
    rank = lax.axis_index("seq")
    col = lax.axis_index("head")
    x = lax.rem(rank, 2)
    z = rank // 2
    partner = rank + 1 - 2 * x

    half_width = half * DH
    near = pl.ds(pl.multiple_of(x * half_width, DH), half_width)
    far = pl.ds(pl.multiple_of((1 - x) * half_width, DH), half_width)
    loads = [
        pltpu.make_async_copy(src, dst, load_sem.at[at])
        for at, (src, dst) in enumerate(
            [
                (ld_hbm, ld_ref),
                (k_hbm.at[:, far], k_ref.at[:, far]),
                (v_hbm.at[:, far], v_ref.at[:, far]),
                (k_hbm.at[:, near], k_ref.at[:, near]),
                (v_hbm.at[:, near], v_ref.at[:, near]),
                (q_hbm, q_ref),
                (g_hbm, g_ref),
            ]
        )
    ]
    for load in loads:
        load.start()

    barrier = pltpu.get_barrier_semaphore()
    pl.semaphore_signal(barrier, inc=1, device_id={"seq": partner})

    @pl.when(z > 0)
    def _():
        pl.semaphore_signal(barrier, inc=1, device_id={"seq": rank - 2})

    @pl.when(z < groups - 1)
    def _():
        pl.semaphore_signal(barrier, inc=1, device_id={"seq": rank + 2})

    for step in range(1, n_head):
        pl.semaphore_signal(barrier, inc=1, device_id={"head": lax.rem(col + step, n_head)})

    def head_at(i):
        return lax.rem(x * half + i, heads)

    def columns(i):
        return pl.ds(pl.multiple_of(head_at(i) * DH, DH), DH)

    def rows(n):
        return pl.ds(n * BLOCK, BLOCK)

    row_ids = lax.broadcasted_iota(jnp.int32, (BLOCK, BLOCK), 0)
    col_ids = lax.broadcasted_iota(jnp.int32, (BLOCK, BLOCK), 1)
    loads[0].wait()
    upto = (row_ids <= col_ids).astype(f32)
    since = (row_ids >= col_ids).astype(f32)
    shard_total = jnp.zeros((heads, BLOCK), f32)
    for n in range(blocks):
        within = lax.dot_general(
            ld_ref[:, rows(n)],
            upto,
            (((1,), (0,)), ((), ())),
            precision=lax.Precision.HIGHEST,
            preferred_element_type=f32,
        )
        total = jnp.broadcast_to(within[:, BLOCK - 1 : BLOCK], (heads, BLOCK))
        by_column = lax.dot_general(
            since,
            ld_ref[:, rows(n)],
            (((1,), (1,)), ((), ())),
            precision=lax.Precision.HIGHEST,
            preferred_element_type=f32,
        )
        for h in range(heads):
            column_ref[h, rows(n)] = jnp.broadcast_to(by_column[:, h : h + 1], (BLOCK, BLOCK))
        within_ref[n] = within
        total_ref[n] = total
        dec_ref[n] = jnp.exp(total)
        shard_total = shard_total + total
    shard_dec_ref[...] = jnp.exp(shard_total)
    loads[1].wait()
    loads[2].wait()

    def pair_copy(d, i, c):
        size = PIECE + 8 if d == 0 else PIECE
        j = i - half
        return pltpu.make_async_remote_copy(
            src_ref=slab.at[d, i, c, pl.ds(0, size)],
            dst_ref=pair_in.at[d, j, c, pl.ds(0, size)],
            send_sem=pair_send.at[d, j, c],
            recv_sem=pair_recv.at[d, j, c],
            device_id={"seq": partner},
        )

    def chain_copy(d, j, c):
        return pltpu.make_async_remote_copy(
            src_ref=chain_out.at[d, j, c],
            dst_ref=chain_in.at[d, j, c],
            send_sem=chain_send.at[d, j, c],
            recv_sem=chain_recv.at[d, j, c],
            device_id={"seq": rank + 2 - 4 * d},
        )

    def fin_copy(d, j, c):
        return pltpu.make_async_remote_copy(
            src_ref=pair_out.at[d, j, c],
            dst_ref=incoming.at[d, half + j, pl.ds(c * PIECE, PIECE)],
            send_sem=fin_send.at[d, j, c],
            recv_sem=fin_recv.at[d, j, c],
            device_id={"seq": partner},
        )

    every = range(blocks)

    def forward_terms(i):
        h = head_at(i)
        at = columns(i)
        to_end = [
            jnp.exp(total_ref[n, pl.ds(h, 1), :] - column_ref[h, rows(n)]) for n in every
        ]
        scaled = [(to_end[n] * k_ref[rows(n), at].astype(f32)).astype(bf16) for n in every]
        term = [dot(scaled[n], v_ref[rows(n), at], 0, 0) for n in every]
        state = term[0]
        for n in every[1:]:
            state = dec_ref[n, pl.ds(h, 1), :] * state + term[n]
        for c in range(CUTS):
            slab[0, i, c, pl.ds(0, PIECE)] = state[c * PIECE : (c + 1) * PIECE]
            slab[0, i, c, pl.ds(PIECE, 8)] = jnp.broadcast_to(
                shard_dec_ref[pl.ds(h, 1), :], (8, DH)
            )
        for n in every:
            end_ref[i, rows(n)] = to_end[n]
            terms[0, i, n] = term[n]

    def forward_inside(i):
        h = head_at(i)
        at = columns(i)
        scores = [dot(q_ref[rows(n), at], k_ref[rows(n), at], 1, 1) for n in every]
        probs = []
        for n in every:
            row = within_ref[n, pl.ds(h, 1), :]
            column = column_ref[h, rows(n)]
            mask = jnp.where(
                row_ids >= col_ids, jnp.exp(jnp.minimum(column - row, 0.0)), 0.0
            )
            probs.append((scores[n] * mask).astype(bf16))
            mask_ref[i, rows(n)] = mask
            grow_ref[i, rows(n)] = jnp.exp(column)
        attn = [dot(probs[n], v_ref[rows(n), at], 1, 0) for n in every]
        for n in every:
            probs_ref[i, rows(n)] = probs[n]
            attn_ref[i, rows(n)] = attn[n]

    def loop(low, high, body):
        def step(i, carry):
            body(i)
            return carry

        lax.fori_loop(low, high, step, 0)

    def scan(d, unit):
        first = (x == 0) if d == 0 else (x == 1)
        at = z if d == 0 else groups - 1 - z

        def step(j):
            for c in range(CUTS):
                pair_copy(d, half + j, c).wait_recv()

                @pl.when(at > 0)
                def _():
                    chain_copy(d, j, c).wait_recv()

                @pl.when(at == 0)
                def _():
                    chain_in[d, j, c] = jnp.zeros((PIECE, DH), f32)

                mine, other = slab[d, j, c, pl.ds(0, PIECE)], pair_in[d, j, c, pl.ds(0, PIECE)]
                mine_dec = slab[0, j, c, pl.ds(PIECE, 1)]
                other_dec = pair_in[0, j, c, pl.ds(PIECE, 1)]
                first_state = jnp.where(first, mine, other)
                last_state = jnp.where(first, other, mine)
                first_dec = jnp.where(first, mine_dec, other_dec)
                last_dec = jnp.where(first, other_dec, mine_dec)
                before = chain_in[d, j, c]
                between = first_dec * before + first_state
                chain_out[d, j, c] = last_dec * between + last_state

                @pl.when(at < groups - 1)
                def _():
                    chain_copy(d, j, c).start()

                incoming[d, j, pl.ds(c * PIECE, PIECE)] = jnp.where(first, before, between)
                pair_out[d, j, c] = jnp.where(first, between, before)
                fin_copy(d, j, c).start()
            unit(j)

        loop(0, half, step)

    n_peers = 1 + (z > 0).astype(jnp.int32) + (z < groups - 1).astype(jnp.int32) + n_head - 1
    pl.semaphore_wait(barrier, n_peers)

    def send_terms(i):
        forward_terms(i)
        for c in range(CUTS):
            pair_copy(0, i, c).start()

    loop(half, heads, send_terms)
    loads[3].wait()
    loads[4].wait()
    loop(0, half, forward_terms)
    loads[5].wait()
    acc_ref[...] = jnp.zeros_like(acc_ref)

    def complete(i):
        h = head_at(i)
        at = columns(i)
        state = incoming[0, i]
        rounded = [state.astype(bf16)]
        for n in every[:-1]:
            state = dec_ref[n, pl.ds(h, 1), :] * state + terms[0, i, n]
            rounded.append(state.astype(bf16))
        inter = [dot(q_ref[rows(n), at], rounded[n], 1, 0) for n in every]
        attn = [attn_ref[i, rows(n)] + grow_ref[i, rows(n)] * inter[n] for n in every]
        square = [acc_ref[0, rows(n)] + attn[n] * attn[n] for n in every]
        cross = [
            acc_ref[1, rows(n)] + attn[n] * g_ref[rows(n), at].astype(f32) for n in every
        ]
        for n in every:
            state_ref[i, n] = rounded[n]
            attn_ref[i, rows(n)] = attn[n]
            acc_ref[0, rows(n)] = square[n]
            acc_ref[1, rows(n)] = cross[n]

    def complete_foreign(i):
        for c in range(CUTS):
            fin_copy(0, i - half, c).wait_recv()
        complete(i)

    def units(ahead, inside, after):
        def unit(j):
            @pl.when(ahead + j < heads)
            def _():
                inside(ahead + j)

            @pl.when(ahead + j >= heads)
            def _():
                after(ahead + j - heads)

        return unit

    def run(d, at, inside, after, after_foreign):
        ahead = (at * heads) // max(groups - 1, 1)
        loop(0, ahead, inside)
        scan(d, units(ahead, inside, after))
        loop(ahead + half, heads, inside)
        loop(jnp.maximum(ahead + half - heads, 0), half, after)
        loop(half, heads, after_foreign)

    loads[6].wait()
    run(0, z, forward_inside, complete, complete_foreign)

    sums = [
        jnp.sum(acc_ref[kind, rows(n)], axis=1, keepdims=True)
        for kind in range(2)
        for n in range(blocks)
    ]
    stat_out[...] = jnp.concatenate(sums, axis=1).T

    def stat_copy(step):
        return pltpu.make_async_remote_copy(
            src_ref=stat_out,
            dst_ref=stat_in.at[step - 1],
            send_sem=stat_send.at[step - 1],
            recv_sem=stat_recv.at[step - 1],
            device_id={"head": lax.rem(col + step, n_head)},
        )

    for step in range(1, n_head):
        stat_copy(step).start()
    stats = stat_out[...]
    for step in range(1, n_head):
        stat_copy(step).wait_recv()
        stats = stats + stat_in[step - 1]
    width = float(HEAD_COUNT * DH)
    inv_rms = lax.rsqrt(stats[:blocks] / width + EPSILON)
    coef = inv_rms * (inv_rms * stats[blocks:] / width)
    scales = jnp.concatenate([inv_rms, coef], axis=0).T
    for kind in range(2):
        for n in range(blocks):
            at = kind * blocks + n
            row_ref[kind, rows(n)] = jnp.broadcast_to(scales[:, at : at + 1], (BLOCK, BLOCK))

    def back_terms(i):
        h = head_at(i)
        at = columns(i)
        scaled = [
            (grow_ref[i, rows(n)] * q_ref[rows(n), at].astype(f32)).astype(bf16) for n in every
        ]
        ag = [
            (
                row_ref[0, rows(n)]
                * (g_ref[rows(n), at].astype(f32) - attn_ref[i, rows(n)] * row_ref[1, rows(n)])
            ).astype(bf16)
            for n in every
        ]
        term = [dot(scaled[n], ag[n], 0, 0) for n in every]
        state = term[-1]
        for n in reversed(every[:-1]):
            state = dec_ref[n, pl.ds(h, 1), :] * state + term[n]
        for c in range(CUTS):
            slab[1, i, c, pl.ds(0, PIECE)] = state[c * PIECE : (c + 1) * PIECE]
        for n in every:
            ag_ref[i, rows(n)] = ag[n]
            terms[1, i, n] = term[n]

    def send_back_terms(i):
        back_terms(i)
        for c in range(CUTS):
            pair_copy(1, i, c).start()

    def out_copy(which, i):
        src, dst = ((q_out, qo_hbm), (k_out, ko_hbm), (v_out, vo_hbm))[which]
        return pltpu.make_async_copy(src.at[i], dst.at[:, columns(i)], out_sem.at[which, i])

    def back_inside(i):
        at = columns(i)
        ag = [ag_ref[i, rows(n)] for n in every]
        inner = [dot(ag[n], v_ref[rows(n), at], 1, 1) for n in every]
        inter = [dot(ag[n], state_ref[i, n], 1, 1) for n in every]
        value = [dot(probs_ref[i, rows(n)], ag[n], 0, 0) for n in every]
        grad = [(inner[n] * mask_ref[i, rows(n)]).astype(bf16) for n in every]
        query = [dot(grad[n], k_ref[rows(n), at], 1, 0) for n in every]
        key = [dot(grad[n], q_ref[rows(n), at], 0, 0) for n in every]
        for n in every:
            q_out[i, rows(n)] = (query[n] + grow_ref[i, rows(n)] * inter[n]).astype(bf16)
            ki_ref[i, rows(n)] = key[n]
            vi_ref[i, rows(n)] = value[n]
        out_copy(0, i).start()

    loop(half, heads, send_back_terms)
    loop(0, half, back_terms)

    def finish(i):
        h = head_at(i)
        at = columns(i)
        state = incoming[1, i]
        rounded = [state.astype(bf16)]
        for n in reversed(every[1:]):
            state = dec_ref[n, pl.ds(h, 1), :] * state + terms[1, i, n]
            rounded.insert(0, state.astype(bf16))
        key = [dot(v_ref[rows(n), at], rounded[n], 1, 1) for n in every]
        value = [dot(k_ref[rows(n), at], rounded[n], 1, 0) for n in every]
        for n in every:
            to_end = end_ref[i, rows(n)]
            k_out[i, rows(n)] = (ki_ref[i, rows(n)] + to_end * key[n]).astype(bf16)
            v_out[i, rows(n)] = (vi_ref[i, rows(n)] + to_end * value[n]).astype(bf16)
        out_copy(1, i).start()
        out_copy(2, i).start()

    def finish_foreign(i):
        for c in range(CUTS):
            fin_copy(1, i - half, c).wait_recv()
        finish(i)

    run(1, groups - 1 - z, back_inside, finish, finish_foreign)

    for step in range(1, n_head):
        stat_copy(step).wait_send()
    for d in range(2):

        def drain(j):
            for c in range(CUTS):
                pair_copy(d, half + j, c).wait_send()
                fin_copy(d, j, c).wait_send()

                @pl.when((z < groups - 1) if d == 0 else (z > 0))
                def _():
                    chain_copy(d, j, c).wait_send()

        loop(0, half, drain)

    def drain_out(i):
        for which in range(3):
            out_copy(which, i).wait()

    loop(0, heads, drain_out)


def write_out(q_in, k_in, v_in, q_hbm, k_hbm, v_hbm, stage, in_sem, out_sem):
    reads, writes = [], []
    for at, (src, dst) in enumerate([(q_in, q_hbm), (k_in, k_hbm), (v_in, v_hbm)]):
        for n in range(src.shape[0] // BLOCK):
            part = pl.ds(n * BLOCK, BLOCK)
            held = stage.at[at, part]
            reads.append(pltpu.make_async_copy(src.at[part], held, in_sem.at[at, n]))
            writes.append(pltpu.make_async_copy(held, dst.at[part], out_sem.at[at, n]))
    for read in reads:
        read.start()
    for read, write in zip(reads, writes):
        read.wait()
        write.start()
    for write in writes:
        write.wait()


def solution(mesh):
    n_seq, n_head = mesh.shape["seq"], mesh.shape["head"]

    def shards(queries, key_rows, value_rows, out_grad, log_decay):
        tokens, width = queries.shape
        heads = log_decay.shape[0]
        blocks = tokens // BLOCK
        half = heads // 2
        full = (heads, tokens, DH)
        dma = pltpu.SemaphoreType.DMA
        scratch = [
            pltpu.VMEM((tokens, width), bf16),
            pltpu.VMEM((tokens, width), bf16),
            pltpu.VMEM((tokens, width), bf16),
            pltpu.VMEM((tokens, width), bf16),
            pltpu.VMEM((heads, tokens), f32),
            pltpu.VMEM((blocks, heads, BLOCK), f32),
            pltpu.VMEM(full, f32),
            pltpu.VMEM((blocks, heads, BLOCK), f32),
            pltpu.VMEM((blocks, heads, BLOCK), f32),
            pltpu.VMEM((heads, BLOCK), f32),
            pltpu.VMEM((2, heads, blocks, DH, DH), f32),
            pltpu.VMEM(full, f32),
            pltpu.VMEM(full, f32),
            pltpu.VMEM(full, f32),
            pltpu.VMEM(full, f32),
            pltpu.VMEM(full, bf16),
            pltpu.VMEM(full, bf16),
            pltpu.VMEM((heads, blocks, DH, DH), bf16),
            pltpu.VMEM(full, f32),
            pltpu.VMEM(full, f32),
            pltpu.VMEM((2, heads, CUTS, PIECE + 8, DH), f32),
            pltpu.VMEM((2, half, CUTS, PIECE + 8, DH), f32),
            pltpu.VMEM((2, half, CUTS, PIECE, DH), f32),
            pltpu.VMEM((2, half, CUTS, PIECE, DH), f32),
            pltpu.VMEM((2, half, CUTS, PIECE, DH), f32),
            pltpu.VMEM((2, heads, DH, DH), f32),
            pltpu.VMEM((2, tokens, DH), f32),
            pltpu.VMEM((2 * blocks, BLOCK), f32),
            pltpu.VMEM((n_head - 1, 2 * blocks, BLOCK), f32),
            pltpu.VMEM((2, tokens, DH), f32),
            pltpu.VMEM(full, bf16),
            pltpu.VMEM(full, bf16),
            pltpu.VMEM(full, bf16),
            dma((7,)),
            dma((2, half, CUTS)),
            dma((2, half, CUTS)),
            dma((2, half, CUTS)),
            dma((2, half, CUTS)),
            dma((2, half, CUTS)),
            dma((2, half, CUTS)),
            dma((n_head - 1,)),
            dma((n_head - 1,)),
            dma((3, heads)),
        ]
        anywhere = pl.BlockSpec(memory_space=pl.ANY)
        in_hbm = pl.BlockSpec(memory_space=pltpu.HBM)
        results = pl.pallas_call(
            functools.partial(kernel, n_seq, n_head),
            out_shape=[jax.ShapeDtypeStruct((tokens, width), bf16)] * 3,
            in_specs=[in_hbm] * 5,
            out_specs=[anywhere] * 3,
            scratch_shapes=scratch,
            compiler_params=pltpu.CompilerParams(
                collective_id=0,
                has_side_effects=True,
                vmem_limit_bytes=VMEM_LIMIT,
            ),
            name="lightning",
        )(queries, key_rows, value_rows, out_grad, log_decay)
        return pl.pallas_call(
            write_out,
            out_shape=[jax.ShapeDtypeStruct((tokens, width), bf16)] * 3,
            in_specs=[anywhere] * 3,
            out_specs=[in_hbm] * 3,
            scratch_shapes=[
                pltpu.VMEM((3, tokens, width), bf16),
                dma((3, blocks)),
                dma((3, blocks)),
            ],
            compiler_params=pltpu.CompilerParams(vmem_limit_bytes=VMEM_LIMIT),
            name="write_out",
        )(*results)

    return jax.shard_map(
        shards,
        mesh=mesh,
        in_specs=(
            P("seq", "head"),
            P("seq", "head"),
            P("seq", "head"),
            P("seq", "head"),
            P("head", "seq"),
        ),
        out_specs=(P("seq", "head"), P("seq", "head"), P("seq", "head")),
        check_vma=False,
    )
```

```python
import functools

import jax
import jax.numpy as jnp
from jax import lax
from jax.experimental import pallas as pl
from jax.experimental.pallas import tpu as pltpu
from jax.sharding import PartitionSpec as P

HEAD_COUNT = 32
DH = 128
BLOCK = 128
CUTS = 2
PIECE = DH // CUTS
VMEM_LIMIT = 61 * 1024 * 1024
EPSILON = 1e-06

f32 = jnp.float32
bf16 = jnp.bfloat16


def dot(left, right, left_dim, right_dim):
    return lax.dot_general(
        left, right, (((left_dim,), (right_dim,)), ((), ())), preferred_element_type=f32
    )


def kernel(
    n_seq,
    n_head,
    q_hbm,
    k_hbm,
    v_hbm,
    g_hbm,
    ld_hbm,
    qo_hbm,
    ko_hbm,
    vo_hbm,
    q_ref,
    k_ref,
    v_ref,
    g_ref,
    ld_ref,
    within_ref,
    column_ref,
    total_ref,
    dec_ref,
    shard_dec_ref,
    terms,
    mask_ref,
    grow_ref,
    end_ref,
    attn_ref,
    probs_ref,
    ag_ref,
    state_ref,
    ki_ref,
    vi_ref,
    slab,
    pair_in,
    chain_in,
    chain_out,
    pair_out,
    incoming,
    acc_ref,
    stat_out,
    stat_in,
    row_ref,
    q_out,
    k_out,
    v_out,
    load_sem,
    pair_send,
    pair_recv,
    chain_send,
    chain_recv,
    fin_send,
    fin_recv,
    stat_send,
    stat_recv,
    out_sem,
):
    heads = ld_ref.shape[0]
    blocks = ld_ref.shape[1] // BLOCK
    half = heads // 2
    groups = n_seq // 2
    rank = lax.axis_index("seq")
    col = lax.axis_index("head")
    x = lax.rem(rank, 2)
    z = rank // 2
    partner = rank + 1 - 2 * x

    half_width = half * DH
    near = pl.ds(pl.multiple_of(x * half_width, DH), half_width)
    far = pl.ds(pl.multiple_of((1 - x) * half_width, DH), half_width)
    loads = [
        pltpu.make_async_copy(src, dst, load_sem.at[at])
        for at, (src, dst) in enumerate(
            [
                (ld_hbm, ld_ref),
                (k_hbm.at[:, far], k_ref.at[:, far]),
                (v_hbm.at[:, far], v_ref.at[:, far]),
                (k_hbm.at[:, near], k_ref.at[:, near]),
                (v_hbm.at[:, near], v_ref.at[:, near]),
                (q_hbm, q_ref),
                (g_hbm, g_ref),
            ]
        )
    ]
    for load in loads:
        load.start()

    barrier = pltpu.get_barrier_semaphore()
    pl.semaphore_signal(barrier, inc=1, device_id={"seq": partner})

    @pl.when(z > 0)
    def _():
        pl.semaphore_signal(barrier, inc=1, device_id={"seq": rank - 2})

    @pl.when(z < groups - 1)
    def _():
        pl.semaphore_signal(barrier, inc=1, device_id={"seq": rank + 2})

    for step in range(1, n_head):
        pl.semaphore_signal(barrier, inc=1, device_id={"head": lax.rem(col + step, n_head)})

    def head_at(i):
        return lax.rem(x * half + i, heads)

    def columns(i):
        return pl.ds(pl.multiple_of(head_at(i) * DH, DH), DH)

    def rows(n):
        return pl.ds(n * BLOCK, BLOCK)

    row_ids = lax.broadcasted_iota(jnp.int32, (BLOCK, BLOCK), 0)
    col_ids = lax.broadcasted_iota(jnp.int32, (BLOCK, BLOCK), 1)
    loads[0].wait()
    upto = (row_ids <= col_ids).astype(bf16)
    since = (row_ids >= col_ids).astype(bf16)
    rest = jnp.concatenate([ld_ref[:, rows(n)] for n in range(blocks)], axis=0)
    parts = []
    for _ in range(3):
        parts.append(rest.astype(bf16))
        rest = rest - parts[-1].astype(f32)
    all_within = sum(dot(part, upto, 1, 0) for part in parts[::-1])
    by_column = sum(dot(since, part, 1, 1) for part in parts[::-1])
    shard_total = jnp.zeros((heads, BLOCK), f32)
    for n in range(blocks):
        within = all_within[n * heads : (n + 1) * heads]
        total = jnp.broadcast_to(within[:, BLOCK - 1 : BLOCK], (heads, BLOCK))
        for h in range(heads):
            lane = n * heads + h
            column_ref[h, rows(n)] = jnp.broadcast_to(
                by_column[:, lane : lane + 1], (BLOCK, BLOCK)
            )
        within_ref[n] = within
        total_ref[n] = total
        dec_ref[n] = jnp.exp(total)
        shard_total = shard_total + total
    shard_dec_ref[...] = jnp.exp(shard_total)
    loads[1].wait()
    loads[2].wait()

    def pair_copy(d, i, c):
        size = PIECE + 8 if d == 0 else PIECE
        j = i - half
        return pltpu.make_async_remote_copy(
            src_ref=slab.at[d, i, c, pl.ds(0, size)],
            dst_ref=pair_in.at[d, j, c, pl.ds(0, size)],
            send_sem=pair_send.at[d, j, c],
            recv_sem=pair_recv.at[d, j, c],
            device_id={"seq": partner},
        )

    def chain_copy(d, j, c):
        return pltpu.make_async_remote_copy(
            src_ref=chain_out.at[d, j, c],
            dst_ref=chain_in.at[d, j, c],
            send_sem=chain_send.at[d, j, c],
            recv_sem=chain_recv.at[d, j, c],
            device_id={"seq": rank + 2 - 4 * d},
        )

    def fin_copy(d, j, c):
        return pltpu.make_async_remote_copy(
            src_ref=pair_out.at[d, j, c],
            dst_ref=incoming.at[d, half + j, pl.ds(c * PIECE, PIECE)],
            send_sem=fin_send.at[d, j, c],
            recv_sem=fin_recv.at[d, j, c],
            device_id={"seq": partner},
        )

    every = range(blocks)

    def forward_terms(i):
        h = head_at(i)
        at = columns(i)
        to_end = [
            jnp.exp(total_ref[n, pl.ds(h, 1), :] - column_ref[h, rows(n)]) for n in every
        ]
        scaled = [(to_end[n] * k_ref[rows(n), at].astype(f32)).astype(bf16) for n in every]
        term = [dot(scaled[n], v_ref[rows(n), at], 0, 0) for n in every]
        state = term[0]
        for n in every[1:]:
            state = dec_ref[n, pl.ds(h, 1), :] * state + term[n]
        for c in range(CUTS):
            slab[0, i, c, pl.ds(0, PIECE)] = state[c * PIECE : (c + 1) * PIECE]
            slab[0, i, c, pl.ds(PIECE, 8)] = jnp.broadcast_to(
                shard_dec_ref[pl.ds(h, 1), :], (8, DH)
            )
        for n in every:
            end_ref[i, rows(n)] = to_end[n]
            terms[0, i, n] = term[n]

    def forward_inside(i):
        h = head_at(i)
        at = columns(i)
        scores = [dot(q_ref[rows(n), at], k_ref[rows(n), at], 1, 1) for n in every]
        probs = []
        for n in every:
            row = within_ref[n, pl.ds(h, 1), :]
            column = column_ref[h, rows(n)]
            mask = jnp.where(
                row_ids >= col_ids, jnp.exp(jnp.minimum(column - row, 0.0)), 0.0
            )
            probs.append((scores[n] * mask).astype(bf16))
            mask_ref[i, rows(n)] = mask
            grow_ref[i, rows(n)] = jnp.exp(column)
        attn = [dot(probs[n], v_ref[rows(n), at], 1, 0) for n in every]
        for n in every:
            probs_ref[i, rows(n)] = probs[n]
            attn_ref[i, rows(n)] = attn[n]

    def loop(low, high, body):
        def step(i, carry):
            body(i)
            return carry

        lax.fori_loop(low, high, step, 0)

    def scan(d, unit):
        first = (x == 0) if d == 0 else (x == 1)
        at = z if d == 0 else groups - 1 - z

        def step(j):
            for c in range(CUTS):
                pair_copy(d, half + j, c).wait_recv()

                @pl.when(at > 0)
                def _():
                    chain_copy(d, j, c).wait_recv()

                @pl.when(at == 0)
                def _():
                    chain_in[d, j, c] = jnp.zeros((PIECE, DH), f32)

                mine, other = slab[d, j, c, pl.ds(0, PIECE)], pair_in[d, j, c, pl.ds(0, PIECE)]
                mine_dec = slab[0, j, c, pl.ds(PIECE, 1)]
                other_dec = pair_in[0, j, c, pl.ds(PIECE, 1)]
                first_state = jnp.where(first, mine, other)
                last_state = jnp.where(first, other, mine)
                first_dec = jnp.where(first, mine_dec, other_dec)
                last_dec = jnp.where(first, other_dec, mine_dec)
                before = chain_in[d, j, c]
                between = first_dec * before + first_state
                chain_out[d, j, c] = last_dec * between + last_state

                @pl.when(at < groups - 1)
                def _():
                    chain_copy(d, j, c).start()

                incoming[d, j, pl.ds(c * PIECE, PIECE)] = jnp.where(first, before, between)
                pair_out[d, j, c] = jnp.where(first, between, before)
                fin_copy(d, j, c).start()
            unit(j)

        loop(0, half, step)

    n_peers = 1 + (z > 0).astype(jnp.int32) + (z < groups - 1).astype(jnp.int32) + n_head - 1
    pl.semaphore_wait(barrier, n_peers)

    def send_terms(i):
        forward_terms(i)
        for c in range(CUTS):
            pair_copy(0, i, c).start()

    loop(half, heads, send_terms)
    loads[3].wait()
    loads[4].wait()
    loop(0, half, forward_terms)
    loads[5].wait()
    acc_ref[...] = jnp.zeros_like(acc_ref)

    def complete(i):
        h = head_at(i)
        at = columns(i)
        state = incoming[0, i]
        rounded = [state.astype(bf16)]
        for n in every[:-1]:
            state = dec_ref[n, pl.ds(h, 1), :] * state + terms[0, i, n]
            rounded.append(state.astype(bf16))
        inter = [dot(q_ref[rows(n), at], rounded[n], 1, 0) for n in every]
        attn = [attn_ref[i, rows(n)] + grow_ref[i, rows(n)] * inter[n] for n in every]
        square = [acc_ref[0, rows(n)] + attn[n] * attn[n] for n in every]
        cross = [
            acc_ref[1, rows(n)] + attn[n] * g_ref[rows(n), at].astype(f32) for n in every
        ]
        for n in every:
            state_ref[i, n] = rounded[n]
            attn_ref[i, rows(n)] = attn[n]
            acc_ref[0, rows(n)] = square[n]
            acc_ref[1, rows(n)] = cross[n]

    def complete_foreign(i):
        for c in range(CUTS):
            fin_copy(0, i - half, c).wait_recv()
        complete(i)

    def units(ahead, inside, after):
        def unit(j):
            @pl.when(ahead + j < heads)
            def _():
                inside(ahead + j)

            @pl.when(ahead + j >= heads)
            def _():
                after(ahead + j - heads)

        return unit

    def run(d, at, inside, after, after_foreign):
        ahead = jnp.minimum(at, heads)
        loop(0, ahead, inside)
        scan(d, units(ahead, inside, after))
        loop(ahead + half, heads, inside)
        loop(jnp.maximum(ahead + half - heads, 0), half, after)
        loop(half, heads, after_foreign)

    loads[6].wait()
    run(0, z, forward_inside, complete, complete_foreign)

    sums = [
        jnp.sum(acc_ref[kind, rows(n)], axis=1, keepdims=True)
        for kind in range(2)
        for n in range(blocks)
    ]
    stat_out[...] = jnp.concatenate(sums, axis=1).T

    def stat_copy(step):
        return pltpu.make_async_remote_copy(
            src_ref=stat_out,
            dst_ref=stat_in.at[step - 1],
            send_sem=stat_send.at[step - 1],
            recv_sem=stat_recv.at[step - 1],
            device_id={"head": lax.rem(col + step, n_head)},
        )

    for step in range(1, n_head):
        stat_copy(step).start()
    stats = stat_out[...]
    for step in range(1, n_head):
        stat_copy(step).wait_recv()
        stats = stats + stat_in[step - 1]
    width = float(HEAD_COUNT * DH)
    inv_rms = lax.rsqrt(stats[:blocks] / width + EPSILON)
    coef = inv_rms * (inv_rms * stats[blocks:] / width)
    scales = jnp.concatenate([inv_rms, coef], axis=0).T
    for kind in range(2):
        for n in range(blocks):
            at = kind * blocks + n
            row_ref[kind, rows(n)] = jnp.broadcast_to(scales[:, at : at + 1], (BLOCK, BLOCK))

    def back_terms(i):
        h = head_at(i)
        at = columns(i)
        scaled = [
            (grow_ref[i, rows(n)] * q_ref[rows(n), at].astype(f32)).astype(bf16) for n in every
        ]
        ag = [
            (
                row_ref[0, rows(n)]
                * (g_ref[rows(n), at].astype(f32) - attn_ref[i, rows(n)] * row_ref[1, rows(n)])
            ).astype(bf16)
            for n in every
        ]
        term = [dot(scaled[n], ag[n], 0, 0) for n in every]
        state = term[-1]
        for n in reversed(every[:-1]):
            state = dec_ref[n, pl.ds(h, 1), :] * state + term[n]
        for c in range(CUTS):
            slab[1, i, c, pl.ds(0, PIECE)] = state[c * PIECE : (c + 1) * PIECE]
        for n in every:
            ag_ref[i, rows(n)] = ag[n]
            terms[1, i, n] = term[n]

    def send_back_terms(i):
        back_terms(i)
        for c in range(CUTS):
            pair_copy(1, i, c).start()

    def out_copy(which, i):
        src, dst = ((q_out, qo_hbm), (k_out, ko_hbm), (v_out, vo_hbm))[which]
        return pltpu.make_async_copy(src.at[i], dst.at[:, columns(i)], out_sem.at[which, i])

    def back_inside(i):
        at = columns(i)
        ag = [ag_ref[i, rows(n)] for n in every]
        inner = [dot(ag[n], v_ref[rows(n), at], 1, 1) for n in every]
        inter = [dot(ag[n], state_ref[i, n], 1, 1) for n in every]
        value = [dot(probs_ref[i, rows(n)], ag[n], 0, 0) for n in every]
        grad = [(inner[n] * mask_ref[i, rows(n)]).astype(bf16) for n in every]
        query = [dot(grad[n], k_ref[rows(n), at], 1, 0) for n in every]
        key = [dot(grad[n], q_ref[rows(n), at], 0, 0) for n in every]
        for n in every:
            q_out[i, rows(n)] = (query[n] + grow_ref[i, rows(n)] * inter[n]).astype(bf16)
            ki_ref[i, rows(n)] = key[n]
            vi_ref[i, rows(n)] = value[n]
        out_copy(0, i).start()

    loop(half, heads, send_back_terms)
    loop(0, half, back_terms)

    def finish(i):
        h = head_at(i)
        at = columns(i)
        state = incoming[1, i]
        rounded = [state.astype(bf16)]
        for n in reversed(every[1:]):
            state = dec_ref[n, pl.ds(h, 1), :] * state + terms[1, i, n]
            rounded.insert(0, state.astype(bf16))
        key = [dot(v_ref[rows(n), at], rounded[n], 1, 1) for n in every]
        value = [dot(k_ref[rows(n), at], rounded[n], 1, 0) for n in every]
        for n in every:
            to_end = end_ref[i, rows(n)]
            k_out[i, rows(n)] = (ki_ref[i, rows(n)] + to_end * key[n]).astype(bf16)
            v_out[i, rows(n)] = (vi_ref[i, rows(n)] + to_end * value[n]).astype(bf16)
        out_copy(1, i).start()
        out_copy(2, i).start()

    def finish_foreign(i):
        for c in range(CUTS):
            fin_copy(1, i - half, c).wait_recv()
        finish(i)

    run(1, groups - 1 - z, back_inside, finish, finish_foreign)

    for step in range(1, n_head):
        stat_copy(step).wait_send()
    for d in range(2):

        def drain(j):
            for c in range(CUTS):
                pair_copy(d, half + j, c).wait_send()
                fin_copy(d, j, c).wait_send()

                @pl.when((z < groups - 1) if d == 0 else (z > 0))
                def _():
                    chain_copy(d, j, c).wait_send()

        loop(0, half, drain)

    def drain_out(i):
        for which in range(3):
            out_copy(which, i).wait()

    loop(0, heads, drain_out)


def write_out(q_in, k_in, v_in, q_hbm, k_hbm, v_hbm, stage, in_sem, out_sem):
    reads, writes = [], []
    for at, (src, dst) in enumerate([(q_in, q_hbm), (k_in, k_hbm), (v_in, v_hbm)]):
        for n in range(src.shape[0] // BLOCK):
            part = pl.ds(n * BLOCK, BLOCK)
            held = stage.at[at, part]
            reads.append(pltpu.make_async_copy(src.at[part], held, in_sem.at[at, n]))
            writes.append(pltpu.make_async_copy(held, dst.at[part], out_sem.at[at, n]))
    for read in reads:
        read.start()
    for read, write in zip(reads, writes):
        read.wait()
        write.start()
    for write in writes:
        write.wait()


def solution(mesh):
    n_seq, n_head = mesh.shape["seq"], mesh.shape["head"]

    def shards(queries, key_rows, value_rows, out_grad, log_decay):
        tokens, width = queries.shape
        heads = log_decay.shape[0]
        blocks = tokens // BLOCK
        half = heads // 2
        full = (heads, tokens, DH)
        dma = pltpu.SemaphoreType.DMA
        scratch = [
            pltpu.VMEM((tokens, width), bf16),
            pltpu.VMEM((tokens, width), bf16),
            pltpu.VMEM((tokens, width), bf16),
            pltpu.VMEM((tokens, width), bf16),
            pltpu.VMEM((heads, tokens), f32),
            pltpu.VMEM((blocks, heads, BLOCK), f32),
            pltpu.VMEM(full, f32),
            pltpu.VMEM((blocks, heads, BLOCK), f32),
            pltpu.VMEM((blocks, heads, BLOCK), f32),
            pltpu.VMEM((heads, BLOCK), f32),
            pltpu.VMEM((2, heads, blocks, DH, DH), f32),
            pltpu.VMEM(full, f32),
            pltpu.VMEM(full, f32),
            pltpu.VMEM(full, f32),
            pltpu.VMEM(full, f32),
            pltpu.VMEM(full, bf16),
            pltpu.VMEM(full, bf16),
            pltpu.VMEM((heads, blocks, DH, DH), bf16),
            pltpu.VMEM(full, f32),
            pltpu.VMEM(full, f32),
            pltpu.VMEM((2, heads, CUTS, PIECE + 8, DH), f32),
            pltpu.VMEM((2, half, CUTS, PIECE + 8, DH), f32),
            pltpu.VMEM((2, half, CUTS, PIECE, DH), f32),
            pltpu.VMEM((2, half, CUTS, PIECE, DH), f32),
            pltpu.VMEM((2, half, CUTS, PIECE, DH), f32),
            pltpu.VMEM((2, heads, DH, DH), f32),
            pltpu.VMEM((2, tokens, DH), f32),
            pltpu.VMEM((2 * blocks, BLOCK), f32),
            pltpu.VMEM((n_head - 1, 2 * blocks, BLOCK), f32),
            pltpu.VMEM((2, tokens, DH), f32),
            pltpu.VMEM(full, bf16),
            pltpu.VMEM(full, bf16),
            pltpu.VMEM(full, bf16),
            dma((7,)),
            dma((2, half, CUTS)),
            dma((2, half, CUTS)),
            dma((2, half, CUTS)),
            dma((2, half, CUTS)),
            dma((2, half, CUTS)),
            dma((2, half, CUTS)),
            dma((n_head - 1,)),
            dma((n_head - 1,)),
            dma((3, heads)),
        ]
        anywhere = pl.BlockSpec(memory_space=pl.ANY)
        in_hbm = pl.BlockSpec(memory_space=pltpu.HBM)
        results = pl.pallas_call(
            functools.partial(kernel, n_seq, n_head),
            out_shape=[jax.ShapeDtypeStruct((tokens, width), bf16)] * 3,
            in_specs=[in_hbm] * 5,
            out_specs=[anywhere] * 3,
            scratch_shapes=scratch,
            compiler_params=pltpu.CompilerParams(
                collective_id=0,
                has_side_effects=True,
                vmem_limit_bytes=VMEM_LIMIT,
            ),
            name="lightning",
        )(queries, key_rows, value_rows, out_grad, log_decay)
        return pl.pallas_call(
            write_out,
            out_shape=[jax.ShapeDtypeStruct((tokens, width), bf16)] * 3,
            in_specs=[anywhere] * 3,
            out_specs=[in_hbm] * 3,
            scratch_shapes=[
                pltpu.VMEM((3, tokens, width), bf16),
                dma((3, blocks)),
                dma((3, blocks)),
            ],
            compiler_params=pltpu.CompilerParams(vmem_limit_bytes=VMEM_LIMIT),
            name="write_out",
        )(*results)

    return jax.shard_map(
        shards,
        mesh=mesh,
        in_specs=(
            P("seq", "head"),
            P("seq", "head"),
            P("seq", "head"),
            P("seq", "head"),
            P("head", "seq"),
        ),
        out_specs=(P("seq", "head"), P("seq", "head"), P("seq", "head")),
        check_vma=False,
    )
```

```python
import functools

import jax
import jax.numpy as jnp
from jax import lax
from jax.experimental import pallas as pl
from jax.experimental.pallas import tpu as pltpu
from jax.sharding import PartitionSpec as P

HEAD_COUNT = 32
DH = 128
BLOCK = 128
CUTS = 2
PIECE = DH // CUTS
VMEM_LIMIT = 61 * 1024 * 1024
EPSILON = 1e-06

f32 = jnp.float32
bf16 = jnp.bfloat16


def dot(left, right, left_dim, right_dim):
    return lax.dot_general(
        left, right, (((left_dim,), (right_dim,)), ((), ())), preferred_element_type=f32
    )


def kernel(
    n_seq,
    n_head,
    q_hbm,
    k_hbm,
    v_hbm,
    g_hbm,
    ld_hbm,
    qo_hbm,
    ko_hbm,
    vo_hbm,
    q_ref,
    k_ref,
    v_ref,
    g_ref,
    ld_ref,
    within_ref,
    column_ref,
    total_ref,
    dec_ref,
    shard_dec_ref,
    terms,
    mask_ref,
    grow_ref,
    end_ref,
    attn_ref,
    probs_ref,
    ag_ref,
    state_ref,
    ki_ref,
    vi_ref,
    slab,
    pair_in,
    chain_in,
    chain_out,
    pair_out,
    incoming,
    acc_ref,
    stat_out,
    stat_in,
    row_ref,
    q_out,
    k_out,
    v_out,
    load_sem,
    pair_send,
    pair_recv,
    chain_send,
    chain_recv,
    fin_send,
    fin_recv,
    stat_send,
    stat_recv,
    out_sem,
):
    heads = ld_ref.shape[0]
    blocks = ld_ref.shape[1] // BLOCK
    half = heads // 2
    groups = n_seq // 2
    rank = lax.axis_index("seq")
    col = lax.axis_index("head")
    x = lax.rem(rank, 2)
    z = rank // 2
    partner = rank + 1 - 2 * x

    half_width = half * DH
    near = pl.ds(pl.multiple_of(x * half_width, DH), half_width)
    far = pl.ds(pl.multiple_of((1 - x) * half_width, DH), half_width)
    loads = [
        pltpu.make_async_copy(src, dst, load_sem.at[at])
        for at, (src, dst) in enumerate(
            [
                (ld_hbm, ld_ref),
                (k_hbm.at[:, far], k_ref.at[:, far]),
                (v_hbm.at[:, far], v_ref.at[:, far]),
                (k_hbm.at[:, near], k_ref.at[:, near]),
                (v_hbm.at[:, near], v_ref.at[:, near]),
                (q_hbm, q_ref),
                (g_hbm, g_ref),
            ]
        )
    ]
    for load in loads:
        load.start()

    barrier = pltpu.get_barrier_semaphore()
    pl.semaphore_signal(barrier, inc=1, device_id={"seq": partner})

    @pl.when(z > 0)
    def _():
        pl.semaphore_signal(barrier, inc=1, device_id={"seq": rank - 2})

    @pl.when(z < groups - 1)
    def _():
        pl.semaphore_signal(barrier, inc=1, device_id={"seq": rank + 2})

    for step in range(1, n_head):
        pl.semaphore_signal(barrier, inc=1, device_id={"head": lax.rem(col + step, n_head)})

    def head_at(i):
        return lax.rem(x * half + i, heads)

    def columns(i):
        return pl.ds(pl.multiple_of(head_at(i) * DH, DH), DH)

    def rows(n):
        return pl.ds(n * BLOCK, BLOCK)

    row_ids = lax.broadcasted_iota(jnp.int32, (BLOCK, BLOCK), 0)
    col_ids = lax.broadcasted_iota(jnp.int32, (BLOCK, BLOCK), 1)
    loads[0].wait()
    upto = (row_ids <= col_ids).astype(bf16)
    since = (row_ids >= col_ids).astype(bf16)
    rest = jnp.concatenate([ld_ref[:, rows(n)] for n in range(blocks)], axis=0)
    parts = []
    for _ in range(3):
        parts.append(rest.astype(bf16))
        rest = rest - parts[-1].astype(f32)
    all_within = sum(dot(part, upto, 1, 0) for part in parts[::-1])
    by_column = sum(dot(since, part, 1, 1) for part in parts[::-1])
    shard_total = jnp.zeros((heads, BLOCK), f32)
    for n in range(blocks):
        within = all_within[n * heads : (n + 1) * heads]
        total = jnp.broadcast_to(within[:, BLOCK - 1 : BLOCK], (heads, BLOCK))
        for h in range(heads):
            lane = n * heads + h
            column_ref[h, rows(n)] = jnp.broadcast_to(
                by_column[:, lane : lane + 1], (BLOCK, BLOCK)
            )
        within_ref[n] = within
        total_ref[n] = total
        dec_ref[n] = jnp.exp(total)
        shard_total = shard_total + total
    shard_dec_ref[...] = jnp.exp(shard_total)

    def pair_copy(d, j, c):
        size = PIECE + 8 if d == 0 else PIECE
        return pltpu.make_async_remote_copy(
            src_ref=slab.at[d, half + j, c, pl.ds(0, size)],
            dst_ref=pair_in.at[d, j, c, pl.ds(0, size)],
            send_sem=pair_send.at[d, j, c],
            recv_sem=pair_recv.at[d, j, c],
            device_id={"seq": partner},
        )

    def chain_copy(d, j, c):
        return pltpu.make_async_remote_copy(
            src_ref=chain_out.at[d, j, c],
            dst_ref=chain_in.at[d, j, c],
            send_sem=chain_send.at[d, j, c],
            recv_sem=chain_recv.at[d, j, c],
            device_id={"seq": rank + 2 - 4 * d},
        )

    def fin_copy(d, j, c):
        return pltpu.make_async_remote_copy(
            src_ref=pair_out.at[d, j, c],
            dst_ref=incoming.at[d, half + j, pl.ds(c * PIECE, PIECE)],
            send_sem=fin_send.at[d, j, c],
            recv_sem=fin_recv.at[d, j, c],
            device_id={"seq": partner},
        )

    every = range(blocks)

    def forward_terms(i):
        h = head_at(i)
        at = columns(i)
        to_end = [
            jnp.exp(total_ref[n, pl.ds(h, 1), :] - column_ref[h, rows(n)]) for n in every
        ]
        scaled = [(to_end[n] * k_ref[rows(n), at].astype(f32)).astype(bf16) for n in every]
        term = [dot(scaled[n], v_ref[rows(n), at], 0, 0) for n in every]
        state = term[0]
        for n in every[1:]:
            state = dec_ref[n, pl.ds(h, 1), :] * state + term[n]
        for c in range(CUTS):
            slab[0, i, c, pl.ds(0, PIECE)] = state[c * PIECE : (c + 1) * PIECE]
            slab[0, i, c, pl.ds(PIECE, 8)] = jnp.broadcast_to(
                shard_dec_ref[pl.ds(h, 1), :], (8, DH)
            )
        for n in every:
            end_ref[i, rows(n)] = to_end[n]
            terms[0, i, n] = term[n]

    def forward_inside(i):
        h = head_at(i)
        at = columns(i)
        scores = [dot(q_ref[rows(n), at], k_ref[rows(n), at], 1, 1) for n in every]
        probs = []
        for n in every:
            row = within_ref[n, pl.ds(h, 1), :]
            column = column_ref[h, rows(n)]
            mask = jnp.where(
                row_ids >= col_ids, jnp.exp(jnp.minimum(column - row, 0.0)), 0.0
            )
            probs.append((scores[n] * mask).astype(bf16))
            mask_ref[i, rows(n)] = mask
            grow_ref[i, rows(n)] = jnp.exp(column)
        attn = [dot(probs[n], v_ref[rows(n), at], 1, 0) for n in every]
        for n in every:
            probs_ref[i, rows(n)] = probs[n]
            attn_ref[i, rows(n)] = attn[n]

    def loop(low, high, body):
        def step(i, carry):
            body(i)
            return carry

        lax.fori_loop(low, high, step, 0)

    def scan(d, unit):
        first = (x == 0) if d == 0 else (x == 1)
        at = z if d == 0 else groups - 1 - z

        def step(j):
            for c in range(CUTS):
                pair_copy(d, j, c).wait_recv()

                @pl.when(at > 0)
                def _():
                    chain_copy(d, j, c).wait_recv()

                @pl.when(at == 0)
                def _():
                    chain_in[d, j, c] = jnp.zeros((PIECE, DH), f32)

                mine, other = slab[d, j, c, pl.ds(0, PIECE)], pair_in[d, j, c, pl.ds(0, PIECE)]
                mine_dec = slab[0, j, c, pl.ds(PIECE, 1)]
                other_dec = pair_in[0, j, c, pl.ds(PIECE, 1)]
                first_state = jnp.where(first, mine, other)
                last_state = jnp.where(first, other, mine)
                first_dec = jnp.where(first, mine_dec, other_dec)
                last_dec = jnp.where(first, other_dec, mine_dec)
                before = chain_in[d, j, c]
                between = first_dec * before + first_state
                chain_out[d, j, c] = last_dec * between + last_state

                @pl.when(at < groups - 1)
                def _():
                    in_turn(chain_copy, d, j, c)

                incoming[d, j, pl.ds(c * PIECE, PIECE)] = jnp.where(first, before, between)
                pair_out[d, j, c] = jnp.where(first, between, before)
                in_turn(fin_copy, d, j, c)
            unit(j)

        loop(0, half, step)

    n_peers = 1 + (z > 0).astype(jnp.int32) + (z < groups - 1).astype(jnp.int32) + n_head - 1
    pl.semaphore_wait(barrier, n_peers)

    def in_turn(copy, d, j, c):
        @pl.when(j > 0)
        def _():
            copy(d, j - 1, c).wait_send()

        copy(d, j, c).start()

    def exchange(d, body):
        def step(j):
            body(half + j)
            for c in range(CUTS):
                in_turn(pair_copy, d, j, c)
            body(j)

        loop(0, half, step)

    for load in loads[1:5]:
        load.wait()
    exchange(0, forward_terms)
    loads[5].wait()
    acc_ref[...] = jnp.zeros_like(acc_ref)

    def complete(i):
        h = head_at(i)
        at = columns(i)
        state = incoming[0, i]
        rounded = [state.astype(bf16)]
        for n in every[:-1]:
            state = dec_ref[n, pl.ds(h, 1), :] * state + terms[0, i, n]
            rounded.append(state.astype(bf16))
        inter = [dot(q_ref[rows(n), at], rounded[n], 1, 0) for n in every]
        attn = [attn_ref[i, rows(n)] + grow_ref[i, rows(n)] * inter[n] for n in every]
        square = [acc_ref[0, rows(n)] + attn[n] * attn[n] for n in every]
        cross = [
            acc_ref[1, rows(n)] + attn[n] * g_ref[rows(n), at].astype(f32) for n in every
        ]
        for n in every:
            state_ref[i, n] = rounded[n]
            attn_ref[i, rows(n)] = attn[n]
            acc_ref[0, rows(n)] = square[n]
            acc_ref[1, rows(n)] = cross[n]

    def complete_foreign(i):
        for c in range(CUTS):
            fin_copy(0, i - half, c).wait_recv()
        complete(i)

    def units(ahead, inside, after):
        def unit(j):
            @pl.when(ahead + j < heads)
            def _():
                inside(ahead + j)

            @pl.when(ahead + j >= heads)
            def _():
                after(ahead + j - heads)

        return unit

    def run(d, at, inside, after, after_foreign):
        ahead = jnp.minimum(at, heads)
        loop(0, ahead, inside)
        scan(d, units(ahead, inside, after))
        loop(ahead + half, heads, inside)
        loop(jnp.maximum(ahead + half - heads, 0), half, after)
        loop(half, heads, after_foreign)

    loads[6].wait()
    run(0, z, forward_inside, complete, complete_foreign)

    sums = [
        jnp.sum(acc_ref[kind, rows(n)], axis=1, keepdims=True)
        for kind in range(2)
        for n in range(blocks)
    ]
    stat_out[...] = jnp.concatenate(sums, axis=1).T

    def stat_copy(step):
        return pltpu.make_async_remote_copy(
            src_ref=stat_out,
            dst_ref=stat_in.at[step - 1],
            send_sem=stat_send.at[step - 1],
            recv_sem=stat_recv.at[step - 1],
            device_id={"head": lax.rem(col + step, n_head)},
        )

    for step in range(1, n_head):
        stat_copy(step).start()
    stats = stat_out[...]
    for step in range(1, n_head):
        stat_copy(step).wait_recv()
        stats = stats + stat_in[step - 1]
    width = float(HEAD_COUNT * DH)
    inv_rms = lax.rsqrt(stats[:blocks] / width + EPSILON)
    coef = inv_rms * (inv_rms * stats[blocks:] / width)
    scales = jnp.concatenate([inv_rms, coef], axis=0).T
    for kind in range(2):
        for n in range(blocks):
            at = kind * blocks + n
            row_ref[kind, rows(n)] = jnp.broadcast_to(scales[:, at : at + 1], (BLOCK, BLOCK))

    def back_terms(i):
        h = head_at(i)
        at = columns(i)
        scaled = [
            (grow_ref[i, rows(n)] * q_ref[rows(n), at].astype(f32)).astype(bf16) for n in every
        ]
        ag = [
            (
                row_ref[0, rows(n)]
                * (g_ref[rows(n), at].astype(f32) - attn_ref[i, rows(n)] * row_ref[1, rows(n)])
            ).astype(bf16)
            for n in every
        ]
        term = [dot(scaled[n], ag[n], 0, 0) for n in every]
        state = term[-1]
        for n in reversed(every[:-1]):
            state = dec_ref[n, pl.ds(h, 1), :] * state + term[n]
        for c in range(CUTS):
            slab[1, i, c, pl.ds(0, PIECE)] = state[c * PIECE : (c + 1) * PIECE]
        for n in every:
            ag_ref[i, rows(n)] = ag[n]
            terms[1, i, n] = term[n]

    def out_copy(which, i):
        src, dst = ((q_out, qo_hbm), (k_out, ko_hbm), (v_out, vo_hbm))[which]
        return pltpu.make_async_copy(src.at[i], dst.at[:, columns(i)], out_sem.at[which, i])

    def back_inside(i):
        at = columns(i)
        ag = [ag_ref[i, rows(n)] for n in every]
        inner = [dot(ag[n], v_ref[rows(n), at], 1, 1) for n in every]
        inter = [dot(ag[n], state_ref[i, n], 1, 1) for n in every]
        value = [dot(probs_ref[i, rows(n)], ag[n], 0, 0) for n in every]
        grad = [(inner[n] * mask_ref[i, rows(n)]).astype(bf16) for n in every]
        query = [dot(grad[n], k_ref[rows(n), at], 1, 0) for n in every]
        key = [dot(grad[n], q_ref[rows(n), at], 0, 0) for n in every]
        for n in every:
            q_out[i, rows(n)] = (query[n] + grow_ref[i, rows(n)] * inter[n]).astype(bf16)
            ki_ref[i, rows(n)] = key[n]
            vi_ref[i, rows(n)] = value[n]
        out_copy(0, i).start()

    exchange(1, back_terms)

    def finish(i):
        h = head_at(i)
        at = columns(i)
        state = incoming[1, i]
        rounded = [state.astype(bf16)]
        for n in reversed(every[1:]):
            state = dec_ref[n, pl.ds(h, 1), :] * state + terms[1, i, n]
            rounded.insert(0, state.astype(bf16))
        key = [dot(v_ref[rows(n), at], rounded[n], 1, 1) for n in every]
        value = [dot(k_ref[rows(n), at], rounded[n], 1, 0) for n in every]
        for n in every:
            to_end = end_ref[i, rows(n)]
            k_out[i, rows(n)] = (ki_ref[i, rows(n)] + to_end * key[n]).astype(bf16)
            v_out[i, rows(n)] = (vi_ref[i, rows(n)] + to_end * value[n]).astype(bf16)
        out_copy(1, i).start()
        out_copy(2, i).start()

    def finish_foreign(i):
        for c in range(CUTS):
            fin_copy(1, i - half, c).wait_recv()
        finish(i)

    run(1, groups - 1 - z, back_inside, finish, finish_foreign)

    for step in range(1, n_head):
        stat_copy(step).wait_send()
    for d in range(2):

        for c in range(CUTS):
            pair_copy(d, half - 1, c).wait_send()
            fin_copy(d, half - 1, c).wait_send()

            @pl.when((z < groups - 1) if d == 0 else (z > 0))
            def _():
                chain_copy(d, half - 1, c).wait_send()

    def drain_out(i):
        for which in range(3):
            out_copy(which, i).wait()

    loop(0, heads, drain_out)


def write_out(q_in, k_in, v_in, q_hbm, k_hbm, v_hbm, stage, in_sem, out_sem):
    reads, writes = [], []
    for at, (src, dst) in enumerate([(q_in, q_hbm), (k_in, k_hbm), (v_in, v_hbm)]):
        for n in range(src.shape[0] // BLOCK):
            part = pl.ds(n * BLOCK, BLOCK)
            held = stage.at[at, part]
            reads.append(pltpu.make_async_copy(src.at[part], held, in_sem.at[at, n]))
            writes.append(pltpu.make_async_copy(held, dst.at[part], out_sem.at[at, n]))
    for read in reads:
        read.start()
    for read, write in zip(reads, writes):
        read.wait()
        write.start()
    for write in writes:
        write.wait()


def solution(mesh):
    n_seq, n_head = mesh.shape["seq"], mesh.shape["head"]

    def shards(queries, key_rows, value_rows, out_grad, log_decay):
        tokens, width = queries.shape
        heads = log_decay.shape[0]
        blocks = tokens // BLOCK
        half = heads // 2
        full = (heads, tokens, DH)
        dma = pltpu.SemaphoreType.DMA
        scratch = [
            pltpu.VMEM((tokens, width), bf16),
            pltpu.VMEM((tokens, width), bf16),
            pltpu.VMEM((tokens, width), bf16),
            pltpu.VMEM((tokens, width), bf16),
            pltpu.VMEM((heads, tokens), f32),
            pltpu.VMEM((blocks, heads, BLOCK), f32),
            pltpu.VMEM(full, f32),
            pltpu.VMEM((blocks, heads, BLOCK), f32),
            pltpu.VMEM((blocks, heads, BLOCK), f32),
            pltpu.VMEM((heads, BLOCK), f32),
            pltpu.VMEM((2, heads, blocks, DH, DH), f32),
            pltpu.VMEM(full, f32),
            pltpu.VMEM(full, f32),
            pltpu.VMEM(full, f32),
            pltpu.VMEM(full, f32),
            pltpu.VMEM(full, bf16),
            pltpu.VMEM(full, bf16),
            pltpu.VMEM((heads, blocks, DH, DH), bf16),
            pltpu.VMEM(full, f32),
            pltpu.VMEM(full, f32),
            pltpu.VMEM((2, heads, CUTS, PIECE + 8, DH), f32),
            pltpu.VMEM((2, half, CUTS, PIECE + 8, DH), f32),
            pltpu.VMEM((2, half, CUTS, PIECE, DH), f32),
            pltpu.VMEM((2, half, CUTS, PIECE, DH), f32),
            pltpu.VMEM((2, half, CUTS, PIECE, DH), f32),
            pltpu.VMEM((2, heads, DH, DH), f32),
            pltpu.VMEM((2, tokens, DH), f32),
            pltpu.VMEM((2 * blocks, BLOCK), f32),
            pltpu.VMEM((n_head - 1, 2 * blocks, BLOCK), f32),
            pltpu.VMEM((2, tokens, DH), f32),
            pltpu.VMEM(full, bf16),
            pltpu.VMEM(full, bf16),
            pltpu.VMEM(full, bf16),
            dma((7,)),
            dma((2, half, CUTS)),
            dma((2, half, CUTS)),
            dma((2, half, CUTS)),
            dma((2, half, CUTS)),
            dma((2, half, CUTS)),
            dma((2, half, CUTS)),
            dma((n_head - 1,)),
            dma((n_head - 1,)),
            dma((3, heads)),
        ]
        anywhere = pl.BlockSpec(memory_space=pl.ANY)
        in_hbm = pl.BlockSpec(memory_space=pltpu.HBM)
        results = pl.pallas_call(
            functools.partial(kernel, n_seq, n_head),
            out_shape=[jax.ShapeDtypeStruct((tokens, width), bf16)] * 3,
            in_specs=[in_hbm] * 5,
            out_specs=[anywhere] * 3,
            scratch_shapes=scratch,
            compiler_params=pltpu.CompilerParams(
                collective_id=0,
                has_side_effects=True,
                vmem_limit_bytes=VMEM_LIMIT,
            ),
            name="lightning",
        )(queries, key_rows, value_rows, out_grad, log_decay)
        return pl.pallas_call(
            write_out,
            out_shape=[jax.ShapeDtypeStruct((tokens, width), bf16)] * 3,
            in_specs=[anywhere] * 3,
            out_specs=[in_hbm] * 3,
            scratch_shapes=[
                pltpu.VMEM((3, tokens, width), bf16),
                dma((3, blocks)),
                dma((3, blocks)),
            ],
            compiler_params=pltpu.CompilerParams(vmem_limit_bytes=VMEM_LIMIT),
            name="write_out",
        )(*results)

    return jax.shard_map(
        shards,
        mesh=mesh,
        in_specs=(
            P("seq", "head"),
            P("seq", "head"),
            P("seq", "head"),
            P("seq", "head"),
            P("head", "seq"),
        ),
        out_specs=(P("seq", "head"), P("seq", "head"), P("seq", "head")),
        check_vma=False,
    )
```

```python
import functools

import jax
import jax.numpy as jnp
from jax import lax
from jax.experimental import pallas as pl
from jax.experimental.pallas import tpu as pltpu
from jax.sharding import PartitionSpec as P

HEAD_COUNT = 32
DH = 128
BLOCK = 128
CUTS = 4
PIECE = DH // CUTS
VMEM_LIMIT = 61 * 1024 * 1024
EPSILON = 1e-06

f32 = jnp.float32
bf16 = jnp.bfloat16


def dot(left, right, left_dim, right_dim):
    return lax.dot_general(
        left, right, (((left_dim,), (right_dim,)), ((), ())), preferred_element_type=f32
    )


def kernel(
    n_seq,
    n_head,
    q_hbm,
    k_hbm,
    v_hbm,
    g_hbm,
    ld_hbm,
    qo_hbm,
    ko_hbm,
    vo_hbm,
    q_ref,
    k_ref,
    v_ref,
    g_ref,
    ld_ref,
    within_ref,
    column_ref,
    total_ref,
    dec_ref,
    shard_dec_ref,
    terms,
    mask_ref,
    grow_ref,
    end_ref,
    attn_ref,
    probs_ref,
    ag_ref,
    state_ref,
    ki_ref,
    vi_ref,
    slab,
    pair_in,
    chain_in,
    chain_out,
    pair_out,
    incoming,
    acc_ref,
    stat_out,
    stat_in,
    row_ref,
    q_out,
    k_out,
    v_out,
    load_sem,
    pair_send,
    pair_recv,
    chain_send,
    chain_recv,
    fin_send,
    fin_recv,
    stat_send,
    stat_recv,
    out_sem,
):
    heads = ld_ref.shape[0]
    blocks = ld_ref.shape[1] // BLOCK
    half = heads // 2
    groups = n_seq // 2
    rank = lax.axis_index("seq")
    col = lax.axis_index("head")
    x = lax.rem(rank, 2)
    z = rank // 2
    partner = rank + 1 - 2 * x

    half_width = half * DH
    near = pl.ds(pl.multiple_of(x * half_width, DH), half_width)
    far = pl.ds(pl.multiple_of((1 - x) * half_width, DH), half_width)
    loads = [
        pltpu.make_async_copy(src, dst, load_sem.at[at])
        for at, (src, dst) in enumerate(
            [
                (ld_hbm, ld_ref),
                (k_hbm.at[:, far], k_ref.at[:, far]),
                (v_hbm.at[:, far], v_ref.at[:, far]),
                (k_hbm.at[:, near], k_ref.at[:, near]),
                (v_hbm.at[:, near], v_ref.at[:, near]),
                (q_hbm, q_ref),
                (g_hbm, g_ref),
            ]
        )
    ]
    for load in loads:
        load.start()

    barrier = pltpu.get_barrier_semaphore()
    pl.semaphore_signal(barrier, inc=1, device_id={"seq": partner})

    @pl.when(z > 0)
    def _():
        pl.semaphore_signal(barrier, inc=1, device_id={"seq": rank - 2})

    @pl.when(z < groups - 1)
    def _():
        pl.semaphore_signal(barrier, inc=1, device_id={"seq": rank + 2})

    for step in range(1, n_head):
        pl.semaphore_signal(barrier, inc=1, device_id={"head": lax.rem(col + step, n_head)})

    def head_at(i):
        return lax.rem(x * half + i, heads)

    def columns(i):
        return pl.ds(pl.multiple_of(head_at(i) * DH, DH), DH)

    def rows(n):
        return pl.ds(n * BLOCK, BLOCK)

    row_ids = lax.broadcasted_iota(jnp.int32, (BLOCK, BLOCK), 0)
    col_ids = lax.broadcasted_iota(jnp.int32, (BLOCK, BLOCK), 1)
    loads[0].wait()
    upto = (row_ids <= col_ids).astype(bf16)
    since = (row_ids >= col_ids).astype(bf16)
    rest = jnp.concatenate([ld_ref[:, rows(n)] for n in range(blocks)], axis=0)
    parts = []
    for _ in range(3):
        parts.append(rest.astype(bf16))
        rest = rest - parts[-1].astype(f32)
    all_within = sum(dot(part, upto, 1, 0) for part in parts[::-1])
    by_column = sum(dot(since, part, 1, 1) for part in parts[::-1])
    shard_total = jnp.zeros((heads, BLOCK), f32)
    for n in range(blocks):
        within = all_within[n * heads : (n + 1) * heads]
        total = jnp.broadcast_to(within[:, BLOCK - 1 : BLOCK], (heads, BLOCK))
        for h in range(heads):
            lane = n * heads + h
            column_ref[h, rows(n)] = jnp.broadcast_to(
                by_column[:, lane : lane + 1], (BLOCK, BLOCK)
            )
        within_ref[n] = within
        total_ref[n] = total
        dec_ref[n] = jnp.exp(total)
        shard_total = shard_total + total
    shard_dec_ref[...] = jnp.exp(shard_total)
    loads[1].wait()
    loads[2].wait()

    def pair_copy(d, i, c):
        size = PIECE + 8 if d == 0 else PIECE
        j = i - half
        return pltpu.make_async_remote_copy(
            src_ref=slab.at[d, i, c, pl.ds(0, size)],
            dst_ref=pair_in.at[d, j, c, pl.ds(0, size)],
            send_sem=pair_send.at[d, j, c],
            recv_sem=pair_recv.at[d, j, c],
            device_id={"seq": partner},
        )

    def chain_copy(d, j, c):
        return pltpu.make_async_remote_copy(
            src_ref=chain_out.at[d, j, c],
            dst_ref=chain_in.at[d, j, c],
            send_sem=chain_send.at[d, j, c],
            recv_sem=chain_recv.at[d, j, c],
            device_id={"seq": rank + 2 - 4 * d},
        )

    def fin_copy(d, j, c):
        return pltpu.make_async_remote_copy(
            src_ref=pair_out.at[d, j, c],
            dst_ref=incoming.at[d, half + j, pl.ds(c * PIECE, PIECE)],
            send_sem=fin_send.at[d, j, c],
            recv_sem=fin_recv.at[d, j, c],
            device_id={"seq": partner},
        )

    every = range(blocks)

    def forward_terms(i):
        h = head_at(i)
        at = columns(i)
        to_end = [
            jnp.exp(total_ref[n, pl.ds(h, 1), :] - column_ref[h, rows(n)]) for n in every
        ]
        scaled = [(to_end[n] * k_ref[rows(n), at].astype(f32)).astype(bf16) for n in every]
        term = [dot(scaled[n], v_ref[rows(n), at], 0, 0) for n in every]
        state = term[0]
        for n in every[1:]:
            state = dec_ref[n, pl.ds(h, 1), :] * state + term[n]
        for c in range(CUTS):
            slab[0, i, c, pl.ds(0, PIECE)] = state[c * PIECE : (c + 1) * PIECE]
            slab[0, i, c, pl.ds(PIECE, 8)] = jnp.broadcast_to(
                shard_dec_ref[pl.ds(h, 1), :], (8, DH)
            )
        for n in every:
            end_ref[i, rows(n)] = to_end[n]
            terms[0, i, n] = term[n]

    def forward_inside(i):
        h = head_at(i)
        at = columns(i)
        scores = [dot(q_ref[rows(n), at], k_ref[rows(n), at], 1, 1) for n in every]
        probs = []
        for n in every:
            row = within_ref[n, pl.ds(h, 1), :]
            column = column_ref[h, rows(n)]
            mask = jnp.where(
                row_ids >= col_ids, jnp.exp(jnp.minimum(column - row, 0.0)), 0.0
            )
            probs.append((scores[n] * mask).astype(bf16))
            mask_ref[i, rows(n)] = mask
            grow_ref[i, rows(n)] = jnp.exp(column)
        attn = [dot(probs[n], v_ref[rows(n), at], 1, 0) for n in every]
        for n in every:
            probs_ref[i, rows(n)] = probs[n]
            attn_ref[i, rows(n)] = attn[n]

    def loop(low, high, body):
        def step(i, carry):
            body(i)
            return carry

        lax.fori_loop(low, high, step, 0)

    def scan(d, unit):
        first = (x == 0) if d == 0 else (x == 1)
        at = z if d == 0 else groups - 1 - z

        def step(j):
            for c in range(CUTS):
                pair_copy(d, half + j, c).wait_recv()

                @pl.when(at > 0)
                def _():
                    chain_copy(d, j, c).wait_recv()

                @pl.when(at == 0)
                def _():
                    chain_in[d, j, c] = jnp.zeros((PIECE, DH), f32)

                mine, other = slab[d, j, c, pl.ds(0, PIECE)], pair_in[d, j, c, pl.ds(0, PIECE)]
                mine_dec = slab[0, j, c, pl.ds(PIECE, 1)]
                other_dec = pair_in[0, j, c, pl.ds(PIECE, 1)]
                first_state = jnp.where(first, mine, other)
                last_state = jnp.where(first, other, mine)
                first_dec = jnp.where(first, mine_dec, other_dec)
                last_dec = jnp.where(first, other_dec, mine_dec)
                before = chain_in[d, j, c]
                between = first_dec * before + first_state
                chain_out[d, j, c] = last_dec * between + last_state

                @pl.when(at < groups - 1)
                def _():
                    chain_copy(d, j, c).start()

                incoming[d, j, pl.ds(c * PIECE, PIECE)] = jnp.where(first, before, between)
                pair_out[d, j, c] = jnp.where(first, between, before)
                fin_copy(d, j, c).start()
            unit(j)

        loop(0, half, step)

    n_peers = 1 + (z > 0).astype(jnp.int32) + (z < groups - 1).astype(jnp.int32) + n_head - 1
    pl.semaphore_wait(barrier, n_peers)

    def send_terms(i):
        forward_terms(i)
        for c in range(CUTS):
            pair_copy(0, i, c).start()

    loop(half, heads, send_terms)
    loads[3].wait()
    loads[4].wait()
    loop(0, half, forward_terms)
    loads[5].wait()
    acc_ref[...] = jnp.zeros_like(acc_ref)

    def complete(i):
        h = head_at(i)
        at = columns(i)
        state = incoming[0, i]
        rounded = [state.astype(bf16)]
        for n in every[:-1]:
            state = dec_ref[n, pl.ds(h, 1), :] * state + terms[0, i, n]
            rounded.append(state.astype(bf16))
        inter = [dot(q_ref[rows(n), at], rounded[n], 1, 0) for n in every]
        attn = [attn_ref[i, rows(n)] + grow_ref[i, rows(n)] * inter[n] for n in every]
        square = [acc_ref[0, rows(n)] + attn[n] * attn[n] for n in every]
        cross = [
            acc_ref[1, rows(n)] + attn[n] * g_ref[rows(n), at].astype(f32) for n in every
        ]
        for n in every:
            state_ref[i, n] = rounded[n]
            attn_ref[i, rows(n)] = attn[n]
            acc_ref[0, rows(n)] = square[n]
            acc_ref[1, rows(n)] = cross[n]

    def complete_foreign(i):
        for c in range(CUTS):
            fin_copy(0, i - half, c).wait_recv()
        complete(i)

    def units(ahead, inside, after):
        def unit(j):
            @pl.when(ahead + j < heads)
            def _():
                inside(ahead + j)

            @pl.when(ahead + j >= heads)
            def _():
                after(ahead + j - heads)

        return unit

    def run(d, at, inside, after, after_foreign):
        ahead = jnp.minimum(at, heads)
        loop(0, ahead, inside)
        scan(d, units(ahead, inside, after))
        loop(ahead + half, heads, inside)
        loop(jnp.maximum(ahead + half - heads, 0), half, after)
        loop(half, heads, after_foreign)

    loads[6].wait()
    run(0, z, forward_inside, complete, complete_foreign)

    sums = [
        jnp.sum(acc_ref[kind, rows(n)], axis=1, keepdims=True)
        for kind in range(2)
        for n in range(blocks)
    ]
    stat_out[...] = jnp.concatenate(sums, axis=1).T

    def stat_copy(step):
        return pltpu.make_async_remote_copy(
            src_ref=stat_out,
            dst_ref=stat_in.at[step - 1],
            send_sem=stat_send.at[step - 1],
            recv_sem=stat_recv.at[step - 1],
            device_id={"head": lax.rem(col + step, n_head)},
        )

    for step in range(1, n_head):
        stat_copy(step).start()
    stats = stat_out[...]
    for step in range(1, n_head):
        stat_copy(step).wait_recv()
        stats = stats + stat_in[step - 1]
    width = float(HEAD_COUNT * DH)
    inv_rms = lax.rsqrt(stats[:blocks] / width + EPSILON)
    coef = inv_rms * (inv_rms * stats[blocks:] / width)
    scales = jnp.concatenate([inv_rms, coef], axis=0).T
    for kind in range(2):
        for n in range(blocks):
            at = kind * blocks + n
            row_ref[kind, rows(n)] = jnp.broadcast_to(scales[:, at : at + 1], (BLOCK, BLOCK))

    def back_terms(i):
        h = head_at(i)
        at = columns(i)
        scaled = [
            (grow_ref[i, rows(n)] * q_ref[rows(n), at].astype(f32)).astype(bf16) for n in every
        ]
        ag = [
            (
                row_ref[0, rows(n)]
                * (g_ref[rows(n), at].astype(f32) - attn_ref[i, rows(n)] * row_ref[1, rows(n)])
            ).astype(bf16)
            for n in every
        ]
        term = [dot(scaled[n], ag[n], 0, 0) for n in every]
        state = term[-1]
        for n in reversed(every[:-1]):
            state = dec_ref[n, pl.ds(h, 1), :] * state + term[n]
        for c in range(CUTS):
            slab[1, i, c, pl.ds(0, PIECE)] = state[c * PIECE : (c + 1) * PIECE]
        for n in every:
            ag_ref[i, rows(n)] = ag[n]
            terms[1, i, n] = term[n]

    def send_back_terms(i):
        back_terms(i)
        for c in range(CUTS):
            pair_copy(1, i, c).start()

    def out_copy(which, i):
        src, dst = ((q_out, qo_hbm), (k_out, ko_hbm), (v_out, vo_hbm))[which]
        return pltpu.make_async_copy(src.at[i], dst.at[:, columns(i)], out_sem.at[which, i])

    def back_inside(i):
        at = columns(i)
        ag = [ag_ref[i, rows(n)] for n in every]
        inner = [dot(ag[n], v_ref[rows(n), at], 1, 1) for n in every]
        inter = [dot(ag[n], state_ref[i, n], 1, 1) for n in every]
        value = [dot(probs_ref[i, rows(n)], ag[n], 0, 0) for n in every]
        grad = [(inner[n] * mask_ref[i, rows(n)]).astype(bf16) for n in every]
        query = [dot(grad[n], k_ref[rows(n), at], 1, 0) for n in every]
        key = [dot(grad[n], q_ref[rows(n), at], 0, 0) for n in every]
        for n in every:
            q_out[i, rows(n)] = (query[n] + grow_ref[i, rows(n)] * inter[n]).astype(bf16)
            ki_ref[i, rows(n)] = key[n]
            vi_ref[i, rows(n)] = value[n]
        out_copy(0, i).start()

    loop(half, heads, send_back_terms)
    loop(0, half, back_terms)

    def finish(i):
        h = head_at(i)
        at = columns(i)
        state = incoming[1, i]
        rounded = [state.astype(bf16)]
        for n in reversed(every[1:]):
            state = dec_ref[n, pl.ds(h, 1), :] * state + terms[1, i, n]
            rounded.insert(0, state.astype(bf16))
        key = [dot(v_ref[rows(n), at], rounded[n], 1, 1) for n in every]
        value = [dot(k_ref[rows(n), at], rounded[n], 1, 0) for n in every]
        for n in every:
            to_end = end_ref[i, rows(n)]
            k_out[i, rows(n)] = (ki_ref[i, rows(n)] + to_end * key[n]).astype(bf16)
            v_out[i, rows(n)] = (vi_ref[i, rows(n)] + to_end * value[n]).astype(bf16)
        out_copy(1, i).start()
        out_copy(2, i).start()

    def finish_foreign(i):
        for c in range(CUTS):
            fin_copy(1, i - half, c).wait_recv()
        finish(i)

    run(1, groups - 1 - z, back_inside, finish, finish_foreign)

    for step in range(1, n_head):
        stat_copy(step).wait_send()
    for d in range(2):

        def drain(j):
            for c in range(CUTS):
                pair_copy(d, half + j, c).wait_send()
                fin_copy(d, j, c).wait_send()

                @pl.when((z < groups - 1) if d == 0 else (z > 0))
                def _():
                    chain_copy(d, j, c).wait_send()

        loop(0, half, drain)

    def drain_out(i):
        for which in range(3):
            out_copy(which, i).wait()

    loop(0, heads, drain_out)


def write_out(q_in, k_in, v_in, q_hbm, k_hbm, v_hbm, stage, in_sem, out_sem):
    reads, writes = [], []
    for at, (src, dst) in enumerate([(q_in, q_hbm), (k_in, k_hbm), (v_in, v_hbm)]):
        for n in range(src.shape[0] // BLOCK):
            part = pl.ds(n * BLOCK, BLOCK)
            held = stage.at[at, part]
            reads.append(pltpu.make_async_copy(src.at[part], held, in_sem.at[at, n]))
            writes.append(pltpu.make_async_copy(held, dst.at[part], out_sem.at[at, n]))
    for read in reads:
        read.start()
    for read, write in zip(reads, writes):
        read.wait()
        write.start()
    for write in writes:
        write.wait()


def solution(mesh):
    n_seq, n_head = mesh.shape["seq"], mesh.shape["head"]

    def shards(queries, key_rows, value_rows, out_grad, log_decay):
        tokens, width = queries.shape
        heads = log_decay.shape[0]
        blocks = tokens // BLOCK
        half = heads // 2
        full = (heads, tokens, DH)
        dma = pltpu.SemaphoreType.DMA
        scratch = [
            pltpu.VMEM((tokens, width), bf16),
            pltpu.VMEM((tokens, width), bf16),
            pltpu.VMEM((tokens, width), bf16),
            pltpu.VMEM((tokens, width), bf16),
            pltpu.VMEM((heads, tokens), f32),
            pltpu.VMEM((blocks, heads, BLOCK), f32),
            pltpu.VMEM(full, f32),
            pltpu.VMEM((blocks, heads, BLOCK), f32),
            pltpu.VMEM((blocks, heads, BLOCK), f32),
            pltpu.VMEM((heads, BLOCK), f32),
            pltpu.VMEM((2, heads, blocks, DH, DH), f32),
            pltpu.VMEM(full, f32),
            pltpu.VMEM(full, f32),
            pltpu.VMEM(full, f32),
            pltpu.VMEM(full, f32),
            pltpu.VMEM(full, bf16),
            pltpu.VMEM(full, bf16),
            pltpu.VMEM((heads, blocks, DH, DH), bf16),
            pltpu.VMEM(full, f32),
            pltpu.VMEM(full, f32),
            pltpu.VMEM((2, heads, CUTS, PIECE + 8, DH), f32),
            pltpu.VMEM((2, half, CUTS, PIECE + 8, DH), f32),
            pltpu.VMEM((2, half, CUTS, PIECE, DH), f32),
            pltpu.VMEM((2, half, CUTS, PIECE, DH), f32),
            pltpu.VMEM((2, half, CUTS, PIECE, DH), f32),
            pltpu.VMEM((2, heads, DH, DH), f32),
            pltpu.VMEM((2, tokens, DH), f32),
            pltpu.VMEM((2 * blocks, BLOCK), f32),
            pltpu.VMEM((n_head - 1, 2 * blocks, BLOCK), f32),
            pltpu.VMEM((2, tokens, DH), f32),
            pltpu.VMEM(full, bf16),
            pltpu.VMEM(full, bf16),
            pltpu.VMEM(full, bf16),
            dma((7,)),
            dma((2, half, CUTS)),
            dma((2, half, CUTS)),
            dma((2, half, CUTS)),
            dma((2, half, CUTS)),
            dma((2, half, CUTS)),
            dma((2, half, CUTS)),
            dma((n_head - 1,)),
            dma((n_head - 1,)),
            dma((3, heads)),
        ]
        anywhere = pl.BlockSpec(memory_space=pl.ANY)
        in_hbm = pl.BlockSpec(memory_space=pltpu.HBM)
        results = pl.pallas_call(
            functools.partial(kernel, n_seq, n_head),
            out_shape=[jax.ShapeDtypeStruct((tokens, width), bf16)] * 3,
            in_specs=[in_hbm] * 5,
            out_specs=[anywhere] * 3,
            scratch_shapes=scratch,
            compiler_params=pltpu.CompilerParams(
                collective_id=0,
                has_side_effects=True,
                vmem_limit_bytes=VMEM_LIMIT,
            ),
            name="lightning",
        )(queries, key_rows, value_rows, out_grad, log_decay)
        return pl.pallas_call(
            write_out,
            out_shape=[jax.ShapeDtypeStruct((tokens, width), bf16)] * 3,
            in_specs=[anywhere] * 3,
            out_specs=[in_hbm] * 3,
            scratch_shapes=[
                pltpu.VMEM((3, tokens, width), bf16),
                dma((3, blocks)),
                dma((3, blocks)),
            ],
            compiler_params=pltpu.CompilerParams(vmem_limit_bytes=VMEM_LIMIT),
            name="write_out",
        )(*results)

    return jax.shard_map(
        shards,
        mesh=mesh,
        in_specs=(
            P("seq", "head"),
            P("seq", "head"),
            P("seq", "head"),
            P("seq", "head"),
            P("head", "seq"),
        ),
        out_specs=(P("seq", "head"), P("seq", "head"), P("seq", "head")),
        check_vma=False,
    )
```
